32 devices in a mesh: depth: 16 (over z, y, x), strip: 2 (over core).
Axes of the slice: x: 2, y: 2, z: 4, core: 2. Of those that a mesh axis runs over, the one named last changes fastest.
Arguments:
- volume: float32 [32, 128, 1024], P('strip', 'depth'), may hold values from -4.5 to 6.5
- extinction: float32 [1], replicated, may hold values from 0.00234375 to 0.0078125
- color_map: float32 [3, 2], replicated, may hold values from -3 to 3
- light_direction: float32 [3], replicated, may hold values from -4 to 4
Outputs:
- image: float32 [4, 32, 1024], P(None, 'strip', 'depth')
The draws below stay inside these ranges and needn't reach their ends.
All inputs are finite; a program needn't handle non-finite values.
Results may differ from the reference program's by a relative error of at most 0.000034.
Values sent between devices are 32-bit elements; how exact they have to be, the bound alone decides.
A program may use at most 64 MiB of HBM per device.

```python
import math
import jax
import jax.numpy as jnp
from jax import lax

ROWS_DEV = 16
DEPTH_DEV = 8
W = 1024
NR = 32
NZ = 128


def draw_volume(key, part):
    offset_key = jax.random.fold_in(key, 11)
    rough_key = jax.random.fold_in(key, 23)
    levels = jax.random.uniform(offset_key, (NR // ROWS_DEV, NZ // DEPTH_DEV), jnp.float32, -0.5, 2.5)
    levels = jnp.repeat(jnp.repeat(levels, ROWS_DEV, axis=0), DEPTH_DEV, axis=1)
    rough_part = jnp.clip(jax.random.normal(rough_key, (NR, NZ, W), jnp.float32), -4.0, 4.0)
    return (levels[:, :, None] + rough_part).astype(jnp.float32)


def draw_light_direction(key, part):
    sign_key = jax.random.fold_in(key, 37)
    size_key = jax.random.fold_in(key, 41)
    signs = jnp.where(jax.random.uniform(sign_key, (3,), jnp.float32) < 0.5, -1.0, 1.0)
    magnitude = jnp.exp(jax.random.uniform(size_key, (3,), jnp.float32, 0.0, 1.3862944))
    return (signs * magnitude).astype(jnp.float32)


def setup_inputs(seed: int = 0) -> dict:
    key_of = jax.random.split(jax.random.key(seed), 5)
    return {
        "volume": draw_volume(jax.random.fold_in(key_of[4], 71), 0),
        "extinction": jnp.clip(jnp.exp(jax.random.uniform(key_of[1], (1,), jnp.float32, math.log(0.00234375), math.log(0.0078125))), 0.00234375, 0.0078125),
        "color_map": jnp.clip(jax.random.uniform(key_of[2], (3, 2), jnp.float32, -3.0, 3.0), -3.0, 3.0),
        "light_direction": draw_light_direction(jax.random.fold_in(key_of[4], 71), 0),
    }


def blur_valid(field_in, along):
    extent = field_in.shape[along]
    lower_cells = lax.slice_in_dim(field_in, 0, extent - 2, axis=along)
    middle = lax.slice_in_dim(field_in, 1, extent - 1, axis=along)
    upper_cells = lax.slice_in_dim(field_in, 2, extent, axis=along)
    return 0.25 * lower_cells + 0.5 * middle + 0.25 * upper_cells


def slope_valid(field_in, along):
    extent = field_in.shape[along]
    lower_cells = lax.slice_in_dim(field_in, 0, extent - 2, axis=along)
    upper_cells = lax.slice_in_dim(field_in, 2, extent, axis=along)
    return 0.5 * (upper_cells - lower_cells)


def smooth_all(padded):
    return blur_valid(blur_valid(blur_valid(padded, 0), 1), 2)


def gradients(padded):
    first = blur_valid(blur_valid(slope_valid(padded, 0), 1), 2)
    second = blur_valid(blur_valid(slope_valid(padded, 1), 0), 2)
    third = blur_valid(blur_valid(slope_valid(padded, 2), 0), 1)
    return first, second, third


def render_slab(smoothed, gradient, extinction, color_map, light_direction):
    facing = gradient[0] * light_direction[0] + gradient[1] * light_direction[1] + gradient[2] * light_direction[2]
    shading = 0.3 + 0.7 * facing * facing / (1.0 + facing * facing)
    optical = extinction[0] * jax.nn.softplus(2.0 * smoothed)
    opacity = 1.0 - jnp.exp(-optical)
    prior_depth = jnp.cumsum(optical, axis=1) - optical
    weights = jnp.exp(-prior_depth) * opacity * shading
    colors = jnp.stack([jnp.sum(weights * jax.nn.sigmoid(color_map[channel, 0] * smoothed + color_map[channel, 1]), axis=1) for channel in range(3)], 0)
    transmit = jnp.exp(-jnp.sum(optical, axis=1))
    return jnp.concatenate([colors, transmit[None]], 0)


def reference(volume, extinction, color_map, light_direction):
    smoothed = smooth_all(jnp.pad(volume, 1))
    gradient = gradients(jnp.pad(smoothed, 1))
    layer = render_slab(smoothed, gradient, extinction, color_map, light_direction)
    return jnp.concatenate([layer[:3], 1.0 - layer[3:]], 0)
```

```python
import functools

import jax
import jax.numpy as jnp
from jax import lax
from jax.experimental import pallas as pl
from jax.experimental.pallas import tpu as pltpu
from jax.sharding import PartitionSpec as P

LANES = 128
EDGE = 8
MESH = pl.DeviceIdType.MESH
SIDES = [(dz, ds) for dz in (-1, 0, 1) for ds in (-1, 0, 1) if (dz, ds) != (0, 0)]


def radices_of(count):
    found = []
    while count > 1:
        radix = 4 if count % 4 == 0 else 2
        found.append(radix)
        count //= radix
    return found


def next_lane(here, after, lane):
    return pltpu.roll(jnp.where(lane == 0, after, here), LANES - 1, here.ndim - 1)


def previous_lane(here, before, lane):
    return pltpu.roll(jnp.where(lane == LANES - 1, before, here), 1, here.ndim - 1)


def place(parts, lane):
    result = None
    for tile, source, target, width in parts:
        shift = (target - source) % LANES
        moved = pltpu.roll(tile, shift, 1) if shift else tile
        if result is None:
            result = moved
        else:
            result = jnp.where((lane >= target) & (lane < target + width), moved, result)
    return result


def plan(groups, columns):
    levels, stride, held = [], 1, columns
    for radix in radices_of(groups):
        levels.append((radix, stride, held, held // radix))
        stride *= radix
        held //= radix
    return levels


def piece_tiles(width):
    if width >= LANES:
        return 1, 4 * (width // LANES)
    per = min(4, LANES // width)
    return per, -(-4 // per)


def kernel(groups, strips, rows, slabs, columns,
           ext_ref, color_ref, light_ref, vol_ref, out_ref,
           vol, ext_field, smooth, ahead, behind, picture, *rest):
    levels = plan(groups, columns)
    sent = rest[:len(levels)]
    got = rest[len(levels):2 * len(levels)]
    load_sem, halo_send, halo_recv, swap_send, swap_recv = rest[2 * len(levels):]
    tiles = columns // LANES
    block = columns // groups
    depth, strip = lax.axis_index("depth"), lax.axis_index("strip")
    lane = lax.broadcasted_iota(jnp.int32, (rows, LANES), 1)
    lane8 = lax.broadcasted_iota(jnp.int32, (8, LANES), 1)
    tall = rows + 8

    loads = [
        pltpu.make_async_copy(vol_ref.at[:, pl.ds(t * LANES, LANES)], vol.at[t], load_sem.at[t])
        for t in range(tiles)
    ]
    for load in loads:
        load.start()

    def there(dz, ds):
        return (depth + dz >= 0) & (depth + dz < groups) & (strip + ds >= 0) & (strip + ds < strips)

    def partner(level, step):
        radix, stride, _, _ = levels[level]
        digit = depth // stride % radix
        other = (digit + step) % radix
        return digit, other, depth + (other - digit) * stride

    barrier = pltpu.get_barrier_semaphore()
    expected = 0
    for dz, ds in SIDES:
        expected = expected + jnp.where(there(dz, ds), 1, 0)

        @pl.when(there(dz, ds))
        def _(dz=dz, ds=ds):
            pl.semaphore_signal(barrier, inc=1, device_id=(depth + dz, strip + ds), device_id_type=MESH)

    for level, (radix, _, _, _) in enumerate(levels):
        for step in range(1, radix):
            pl.semaphore_signal(
                barrier, inc=1, device_id=(partner(level, step)[2], strip), device_id_type=MESH
            )
            expected = expected + 1

    @pl.when(depth == 0)
    def _():
        ext_field[:, 0:2] = jnp.zeros((tiles, 2, rows + 2 * EDGE, LANES), jnp.float32)

    @pl.when(depth == groups - 1)
    def _():
        ext_field[:, slabs + 2:] = jnp.zeros((tiles, 2, rows + 2 * EDGE, LANES), jnp.float32)

    @pl.when(strip == 0)
    def _():
        ext_field[:, :, 0:EDGE] = jnp.zeros((tiles, slabs + 4, EDGE, LANES), jnp.float32)

    @pl.when(strip == strips - 1)
    def _():
        ext_field[:, :, rows + EDGE:] = jnp.zeros((tiles, slabs + 4, EDGE, LANES), jnp.float32)

    ahead[tiles] = jnp.zeros((slabs, rows, LANES), jnp.float32)
    behind[0] = jnp.zeros((slabs, rows, LANES), jnp.float32)

    for load in loads:
        load.wait()

    def blur_columns(z, carry):
        for h in range(rows // 8):
            cells = [vol[t, pl.ds(8 * h * slabs + z, 8, stride=slabs), :] for t in range(tiles)]
            nothing = jnp.zeros_like(cells[0])
            for t in range(tiles):
                before = cells[t - 1] if t > 0 else nothing
                after = cells[t + 1] if t < tiles - 1 else nothing
                ext_field[t, z + 2, EDGE + 8 * h:EDGE + 8 * h + 8] = (
                    next_lane(cells[t], after, lane8)
                    + previous_lane(cells[t], before, lane8)
                    + 2.0 * cells[t]
                )
        return carry

    lax.fori_loop(0, slabs, blur_columns, 0)
    pl.semaphore_wait(barrier, expected)

    first = levels[0]
    stages = max(1, first[3] // LANES)
    per_stage = tiles // stages
    ends = [min(tiles, (c + 1) * per_stage + 1) for c in range(stages)]
    starts = [0] + ends[:-1]

    def halo(c, index, sender):
        dz, ds = SIDES[index]
        span = pl.ds(starts[c], ends[c] - starts[c])
        z_from, z_to, z_count = {
            -1: (2, slabs + 2, 2), 0: (2, 2, slabs), 1: (slabs, 0, 2)}[dz]
        r_from, r_to, r_count = {
            -1: (EDGE, EDGE + rows, 2), 0: (EDGE, EDGE, rows), 1: (EDGE + rows - 2, EDGE - 2, 2)}[ds]
        sign = 1 if sender else -1
        return pltpu.make_async_remote_copy(
            src_ref=ext_field.at[span, pl.ds(z_from, z_count), pl.ds(r_from, r_count)],
            dst_ref=ext_field.at[span, pl.ds(z_to, z_count), pl.ds(r_to, r_count)],
            send_sem=halo_send.at[c, index],
            recv_sem=halo_recv.at[c, index],
            device_id=(depth + sign * dz, strip + sign * ds),
            device_id_type=MESH,
        )

    for c in range(stages):
        for index, (dz, ds) in enumerate(SIDES):
            @pl.when(there(dz, ds))
            def _(c=c, index=index):
                halo(c, index, True).start()

    row = lax.broadcasted_iota(jnp.int32, (tall, LANES), 0)
    inside = ((row > 0) | (strip > 0)) & ((row != rows + 1) | (strip < strips - 1))
    scale = jnp.where(inside, 1.0 / 64.0, 0.0)
    scale_front = jnp.where(inside & (depth > 0), 1.0 / 64.0, 0.0)
    scale_back = jnp.where(inside & (depth < groups - 1), 1.0 / 64.0, 0.0)
    light = [light_ref[0] / 32.0, light_ref[1] / 32.0, light_ref[2] / 32.0]

    def gradients(t, carry):
        def over_rows(z):
            return (
                ext_field[t, z, EDGE - 2:EDGE - 2 + tall]
                + ext_field[t, z, EDGE:EDGE + tall]
                + 2.0 * ext_field[t, z, EDGE - 1:EDGE - 1 + tall]
            )

        one, two = over_rows(0), over_rows(1)
        for z in range(slabs + 2):
            three = over_rows(z + 2)
            weight = scale_front if z == 0 else scale_back if z == slabs + 1 else scale
            smooth[t, z] = jnp.where(weight > 0.0, (one + three + 2.0 * two) * weight, 0.0)
            one, two = two, three

        def rows_of(z):
            low = smooth[t, z, 0:rows]
            middle = smooth[t, z, 1:rows + 1]
            high = smooth[t, z, 2:rows + 2]
            return low + high + 2.0 * middle, high - low

        sums, slopes = zip(*[rows_of(0), rows_of(1)])
        sums, slopes = list(sums), list(slopes)
        for z in range(slabs):
            more, steeper = rows_of(z + 2)
            sums.append(more)
            slopes.append(steeper)
            across = (
                light[0] * (slopes[z] + slopes[z + 2] + 2.0 * slopes[z + 1])
                + light[1] * (sums[z + 2] - sums[z])
            )
            along = light[2] * (sums[z] + sums[z + 2] + 2.0 * sums[z + 1])
            ahead[t, z] = across + along
            behind[t + 1, z] = across - along
        return carry

    extinction = ext_ref[0]
    slope = [0.5 * color_ref[k, 0] for k in range(3)]
    offset = [0.5 * color_ref[k, 1] for k in range(3)]

    def render(t, carry):
        optical = jnp.zeros((rows, LANES), jnp.float32)
        passed = jnp.ones((rows, LANES), jnp.float32)
        total = jnp.zeros((rows, LANES), jnp.float32)
        tinted = [jnp.zeros((rows, LANES), jnp.float32) for _ in range(3)]
        for z in range(slabs):
            up, down = ahead[t, z], behind[t + 1, z]
            facing = (
                next_lane(up, ahead[t + 1, z], lane)
                + previous_lane(down, behind[t, z], lane)
                + (up + down)
            )
            shading = 1.0 - 0.7 * pl.reciprocal(1.0 + facing * facing)
            field = smooth[t, z + 1, 1:rows + 1]
            double = 2.0 * field
            optical += extinction * (
                jnp.maximum(double, 0.0) + jnp.log1p(jnp.exp(-jnp.abs(double)))
            )
            beyond = jnp.exp(-optical)
            weight = (passed - beyond) * shading
            passed = beyond
            total += weight
            for k in range(3):
                tinted[k] += weight * jnp.tanh(slope[k] * field + offset[k])
        for k in range(3):
            picture[t, k] = 0.5 * (total + tinted[k])
        picture[t, 3] = passed
        return carry

    def swap(level, step, part, sender):
        digit, other, target = partner(level, step if sender else -step)
        source, slot = (other, digit) if sender else (digit, other)
        return pltpu.make_async_remote_copy(
            src_ref=sent[level].at[source, part],
            dst_ref=got[level].at[slot, part],
            send_sem=swap_send.at[level, step - 1, part],
            recv_sem=swap_recv.at[level, step - 1, part],
            device_id=(target, strip),
            device_id_type=MESH,
        )

    def dispatch(level, part):
        radix = levels[level][0]
        for step in range(1, radix):
            swap(level, step, part, True).start()
        digit = partner(level, 1)[0]
        got[level][digit, part] = sent[level][digit, part]

    def fill(level, part, tile_of):
        radix, _, held, width = levels[level]
        per, count = piece_tiles(width)
        for j in range(radix):
            blocks = [q * radix + j for q in range(width // block)]
            if width >= LANES:
                each = LANES // block
                blocks = blocks[part * each:(part + 1) * each]
                for k in range(4):
                    sent[level][j, part, k] = place(
                        [
                            (tile_of(k, b * block // LANES), b * block % LANES, i * block, block)
                            for i, b in enumerate(blocks)
                        ],
                        lane,
                    )
            else:
                for c in range(count):
                    sent[level][j, part, c] = place(
                        [
                            (
                                tile_of(k, b * block // LANES), b * block % LANES,
                                (k - c * per) * width + i * block, block,
                            )
                            for k in range(c * per, min(4, (c + 1) * per))
                            for i, b in enumerate(blocks)
                        ],
                        lane,
                    )

    for c in range(stages):
        for index, (dz, ds) in enumerate(SIDES):
            @pl.when(there(-dz, -ds))
            def _(c=c, index=index):
                halo(c, index, False).wait_recv()

        lax.fori_loop(starts[c], ends[c], gradients, 0)
        lax.fori_loop(c * per_stage, (c + 1) * per_stage, render, 0)
        fill(0, c, lambda k, t: picture[t, k])
        dispatch(0, c)

    current = None
    for level, (radix, _, held, width) in enumerate(levels):
        parts = max(1, width // LANES)
        if level > 0:
            for part in range(parts):
                fill(level, part, lambda k, t: current[t][k])
                dispatch(level, part)
        per, _ = piece_tiles(width)
        merged = []
        for part in range(parts):
            for step in range(1, radix):
                swap(level, step, part, False).wait_recv()

            def channel(j, k):
                tile = got[level][j, part, k // per]
                shift = -(k % per) * width % LANES
                return pltpu.roll(tile, shift, 1) if shift else tile

            value = [channel(0, k) for k in range(4)]
            for j in range(1, radix):
                value = [value[k] + value[3] * channel(j, k) for k in range(3)] + [
                    value[3] * channel(j, 3)
                ]
            merged.append(value)
        current = merged

    for k in range(4):
        out_ref[k] = current[0][k][:, :block]

    for c in range(stages):
        for index, (dz, ds) in enumerate(SIDES):
            @pl.when(there(dz, ds))
            def _(c=c, index=index):
                halo(c, index, True).wait_send()
    for level, (radix, _, _, width) in enumerate(levels):
        for part in range(max(1, width // LANES)):
            for step in range(1, radix):
                swap(level, step, part, True).wait_send()


def local(volume, extinction, color_map, light_direction):
    rows, slabs, columns = volume.shape
    groups, strips = lax.axis_size("depth"), lax.axis_size("strip")
    tiles, block = columns // LANES, columns // groups
    levels = plan(groups, columns)
    stages = max(1, levels[0][3] // LANES)
    f32 = jnp.float32
    buffers = []
    for radix, _, _, width in levels:
        parts = max(1, width // LANES)
        buffers.append(pltpu.VMEM((radix, parts, piece_tiles(width)[1] // parts, rows, LANES), f32))
    most = max(max(1, width // LANES) for _, _, _, width in levels)
    image = pl.pallas_call(
        functools.partial(kernel, groups, strips, rows, slabs, columns),
        out_shape=jax.ShapeDtypeStruct((4, rows, block), f32),
        in_specs=[pl.BlockSpec(memory_space=pltpu.SMEM)] * 3 + [pl.BlockSpec(memory_space=pl.ANY)],
        out_specs=pl.BlockSpec(memory_space=pltpu.VMEM),
        scratch_shapes=[
            pltpu.VMEM((tiles, rows * slabs, LANES), f32),
            pltpu.VMEM((tiles, slabs + 4, rows + 2 * EDGE, LANES), f32),
            pltpu.VMEM((tiles, slabs + 2, rows + 8, LANES), f32),
            pltpu.VMEM((tiles + 1, slabs, rows, LANES), f32),
            pltpu.VMEM((tiles + 1, slabs, rows, LANES), f32),
            pltpu.VMEM((tiles, 4, rows, LANES), f32),
            *buffers,
            *buffers,
            pltpu.SemaphoreType.DMA((tiles,)),
            pltpu.SemaphoreType.DMA((stages, len(SIDES))),
            pltpu.SemaphoreType.DMA((stages, len(SIDES))),
            pltpu.SemaphoreType.DMA((len(levels), 3, most)),
            pltpu.SemaphoreType.DMA((len(levels), 3, most)),
        ],
        compiler_params=pltpu.CompilerParams(
            collective_id=0, has_side_effects=True, vmem_limit_bytes=32 * 1024 * 1024
        ),
    )(extinction, color_map, light_direction, volume.reshape(rows * slabs, columns))
    last = lax.broadcasted_iota(jnp.int32, image.shape, 0) == 3
    return jnp.where(last, 1.0 - image, image)


def solution(mesh):
    in_specs = (P("strip", "depth", None), P(), P(), P())
    out_specs = P(None, "strip", "depth")
    return jax.shard_map(local, mesh=mesh, in_specs=in_specs, out_specs=out_specs, check_vma=False)
```

```python
import functools

import jax
import jax.numpy as jnp
from jax import lax
from jax.experimental import pallas as pl
from jax.experimental.pallas import tpu as pltpu
from jax.sharding import PartitionSpec as P

LANES = 128
EDGE = 8
MESH = pl.DeviceIdType.MESH
SIDES = [(dz, ds) for dz in (-1, 0, 1) for ds in (-1, 0, 1) if (dz, ds) != (0, 0)]


def radices_of(count):
    found = []
    while count > 1:
        radix = 4 if count % 4 == 0 else 2
        found.append(radix)
        count //= radix
    return found


def next_lane(here, after, lane):
    return pltpu.roll(jnp.where(lane == 0, after, here), LANES - 1, here.ndim - 1)


def previous_lane(here, before, lane):
    return pltpu.roll(jnp.where(lane == LANES - 1, before, here), 1, here.ndim - 1)


def place(parts, lane):
    result = None
    for tile, source, target, width in parts:
        shift = (target - source) % LANES
        moved = pltpu.roll(tile, shift, 1) if shift else tile
        if result is None:
            result = moved
        else:
            result = jnp.where((lane >= target) & (lane < target + width), moved, result)
    return result


def plan(groups, columns):
    levels, stride, held = [], 1, columns
    for radix in radices_of(groups):
        levels.append((radix, stride, held, held // radix))
        stride *= radix
        held //= radix
    return levels


def piece_tiles(width):
    if width >= LANES:
        return 1, 4 * (width // LANES)
    per = min(4, LANES // width)
    return per, -(-4 // per)


def kernel(groups, strips, rows, slabs, columns,
           ext_hbm, color_hbm, light_hbm, vol_ref, out_ref,
           ext_ref, color_ref, light_ref, vol, ext_field, smooth, ahead, behind, picture, *rest):
    levels = plan(groups, columns)
    sent = rest[:len(levels)]
    got = rest[len(levels):2 * len(levels)]
    load_sem, small_sem, halo_send, halo_recv, swap_send, swap_recv = rest[2 * len(levels):]
    tiles = columns // LANES
    block = columns // groups
    depth, strip = lax.axis_index("depth"), lax.axis_index("strip")
    lane = lax.broadcasted_iota(jnp.int32, (rows, LANES), 1)
    lane8 = lax.broadcasted_iota(jnp.int32, (8, LANES), 1)
    tall = rows + 8

    loads = [
        pltpu.make_async_copy(vol_ref.at[:, pl.ds(t * LANES, LANES)], vol.at[t], load_sem.at[t])
        for t in range(tiles)
    ]
    for load in loads:
        load.start()
    scalars = [
        pltpu.make_async_copy(source, target, small_sem.at[i])
        for i, (source, target) in enumerate(
            [(ext_hbm, ext_ref), (color_hbm, color_ref), (light_hbm, light_ref)])
    ]
    for scalar in scalars:
        scalar.start()

    def there(dz, ds):
        return (depth + dz >= 0) & (depth + dz < groups) & (strip + ds >= 0) & (strip + ds < strips)

    def partner(level, step):
        radix, stride, _, _ = levels[level]
        digit = depth // stride % radix
        other = (digit + step) % radix
        return digit, other, depth + (other - digit) * stride

    barrier = pltpu.get_barrier_semaphore()
    expected = 0
    for dz, ds in SIDES:
        expected = expected + jnp.where(there(dz, ds), 1, 0)

        @pl.when(there(dz, ds))
        def _(dz=dz, ds=ds):
            pl.semaphore_signal(barrier, inc=1, device_id=(depth + dz, strip + ds), device_id_type=MESH)

    for level, (radix, _, _, _) in enumerate(levels):
        for step in range(1, radix):
            pl.semaphore_signal(
                barrier, inc=1, device_id=(partner(level, step)[2], strip), device_id_type=MESH
            )
            expected = expected + 1

    @pl.when(depth == 0)
    def _():
        ext_field[:, 0:2] = jnp.zeros((tiles, 2, rows + 2 * EDGE, LANES), jnp.float32)

    @pl.when(depth == groups - 1)
    def _():
        ext_field[:, slabs + 2:] = jnp.zeros((tiles, 2, rows + 2 * EDGE, LANES), jnp.float32)

    @pl.when(strip == 0)
    def _():
        ext_field[:, :, 0:EDGE] = jnp.zeros((tiles, slabs + 4, EDGE, LANES), jnp.float32)

    @pl.when(strip == strips - 1)
    def _():
        ext_field[:, :, rows + EDGE:] = jnp.zeros((tiles, slabs + 4, EDGE, LANES), jnp.float32)

    ahead[tiles] = jnp.zeros((slabs, rows, LANES), jnp.float32)
    behind[0] = jnp.zeros((slabs, rows, LANES), jnp.float32)

    for load in loads:
        load.wait()

    first = levels[0]
    stages = max(1, first[3] // LANES)
    per_stage = tiles // stages
    ends = [min(tiles, (c + 1) * per_stage + 1) for c in range(stages)]
    starts = [0] + ends[:-1]

    def halo(c, index, sender):
        dz, ds = SIDES[index]
        span = pl.ds(starts[c], ends[c] - starts[c])
        z_from, z_to, z_count = {
            -1: (2, slabs + 2, 2), 0: (2, 2, slabs), 1: (slabs, 0, 2)}[dz]
        r_from, r_to, r_count = {
            -1: (EDGE, EDGE + rows, 2), 0: (EDGE, EDGE, rows), 1: (EDGE + rows - 2, EDGE - 2, 2)}[ds]
        sign = 1 if sender else -1
        return pltpu.make_async_remote_copy(
            src_ref=ext_field.at[span, pl.ds(z_from, z_count), pl.ds(r_from, r_count)],
            dst_ref=ext_field.at[span, pl.ds(z_to, z_count), pl.ds(r_to, r_count)],
            send_sem=halo_send.at[c, index],
            recv_sem=halo_recv.at[c, index],
            device_id=(depth + sign * dz, strip + sign * ds),
            device_id_type=MESH,
        )

    def blur_columns(z, carry):
        for h in range(rows // 8):
            cells = [vol[t, pl.ds(8 * h * slabs + z, 8, stride=slabs), :] for t in range(tiles)]
            nothing = jnp.zeros_like(cells[0])
            for t in range(tiles):
                before = cells[t - 1] if t > 0 else nothing
                after = cells[t + 1] if t < tiles - 1 else nothing
                ext_field[t, z + 2, EDGE + 8 * h:EDGE + 8 * h + 8] = (
                    next_lane(cells[t], after, lane8)
                    + previous_lane(cells[t], before, lane8)
                    + 2.0 * cells[t]
                )
        return carry

    def start_halos(chosen):
        for c in range(stages):
            for index in chosen:
                dz, ds = SIDES[index]

                @pl.when(there(dz, ds))
                def _(c=c, index=index):
                    halo(c, index, True).start()

    def wait_halos(c, chosen):
        for index in chosen:
            dz, ds = SIDES[index]

            @pl.when(there(-dz, -ds))
            def _(c=c, index=index):
                halo(c, index, False).wait_recv()

    over_depth = [i for i, (dz, _) in enumerate(SIDES) if dz != 0]
    over_strip = [i for i, (dz, _) in enumerate(SIDES) if dz == 0]
    lax.fori_loop(0, 2, blur_columns, 0)
    lax.fori_loop(slabs - 2, slabs, blur_columns, 0)
    pl.semaphore_wait(barrier, expected)
    start_halos(over_depth)
    lax.fori_loop(2, slabs - 2, blur_columns, 0)
    start_halos(over_strip)

    row = lax.broadcasted_iota(jnp.int32, (tall, LANES), 0)
    inside = ((row > 0) | (strip > 0)) & ((row != rows + 1) | (strip < strips - 1))
    scale = jnp.where(inside, 1.0 / 64.0, 0.0)
    scale_front = jnp.where(inside & (depth > 0), 1.0 / 64.0, 0.0)
    scale_back = jnp.where(inside & (depth < groups - 1), 1.0 / 64.0, 0.0)
    for scalar in scalars:
        scalar.wait()
    light = [light_ref[0] / 32.0, light_ref[1] / 32.0, light_ref[2] / 32.0]

    def smooth_slices(t, low, high):
        def over_rows(z):
            return (
                ext_field[t, z, EDGE - 2:EDGE - 2 + tall]
                + ext_field[t, z, EDGE:EDGE + tall]
                + 2.0 * ext_field[t, z, EDGE - 1:EDGE - 1 + tall]
            )

        one, two = over_rows(low), over_rows(low + 1)
        for z in range(low, high):
            three = over_rows(z + 2)
            weight = scale_front if z == 0 else scale_back if z == slabs + 1 else scale
            smooth[t, z] = jnp.where(weight > 0.0, (one + three + 2.0 * two) * weight, 0.0)
            one, two = two, three

    def gradients(t, low, high):
        def rows_of(z):
            under = smooth[t, z, 0:rows]
            middle = smooth[t, z, 1:rows + 1]
            over = smooth[t, z, 2:rows + 2]
            return under + over + 2.0 * middle, over - under

        one, two = rows_of(low), rows_of(low + 1)
        for z in range(low, high):
            three = rows_of(z + 2)
            across = (
                light[0] * (one[1] + three[1] + 2.0 * two[1])
                + light[1] * (three[0] - one[0])
            )
            along = light[2] * (one[0] + three[0] + 2.0 * two[0])
            ahead[t, z] = across + along
            behind[t + 1, z] = across - along
            one, two = two, three

    extinction = ext_ref[0]
    slope = [0.5 * color_ref[0, k] for k in range(3)]
    offset = [0.5 * color_ref[1, k] for k in range(3)]

    def render(t, low, high):
        optical = jnp.zeros((rows, LANES), jnp.float32)
        passed = jnp.ones((rows, LANES), jnp.float32)
        total = jnp.zeros((rows, LANES), jnp.float32)
        tinted = [jnp.zeros((rows, LANES), jnp.float32) for _ in range(3)]
        for z in range(low, high):
            up, down = ahead[t, z], behind[t + 1, z]
            facing = (
                next_lane(up, ahead[t + 1, z], lane)
                + previous_lane(down, behind[t, z], lane)
                + (up + down)
            )
            shading = 1.0 - 0.7 * pl.reciprocal(1.0 + facing * facing)
            field = smooth[t, z + 1, 1:rows + 1]
            double = 2.0 * field
            optical += extinction * (
                jnp.maximum(double, 0.0) + jnp.log1p(jnp.exp(-jnp.abs(double)))
            )
            beyond = jnp.exp(-optical)
            weight = (passed - beyond) * shading
            passed = beyond
            total += weight
            for k in range(3):
                tinted[k] += weight * jnp.tanh(slope[k] * field + offset[k])
        return [0.5 * (total + tinted[k]) for k in range(3)] + [passed]

    def over(front, back):
        return [front[k] + front[3] * back[k] for k in range(3)] + [front[3] * back[3]]

    inner = (2, max(2, slabs - 2))

    def inner_field(t, carry):
        smooth_slices(t, inner[0], inner[1] + 2)
        gradients(t, *inner)
        return carry

    def inner_render(t, carry):
        value = render(t, *inner)
        for k in range(4):
            picture[t, k] = value[k]
        return carry

    def outer_field(t, carry):
        smooth_slices(t, 0, inner[0])
        smooth_slices(t, inner[1] + 2, slabs + 2)
        gradients(t, 0, inner[0])
        gradients(t, inner[1], slabs)
        return carry

    def outer_render(t, carry):
        value = over(render(t, 0, inner[0]), [picture[t, k] for k in range(4)])
        value = over(value, render(t, inner[1], slabs))
        for k in range(4):
            picture[t, k] = value[k]
        return carry

    def swap(level, step, part, sender):
        digit, other, target = partner(level, step if sender else -step)
        source, slot = (other, digit) if sender else (digit, other)
        return pltpu.make_async_remote_copy(
            src_ref=sent[level].at[source, part],
            dst_ref=got[level].at[slot, part],
            send_sem=swap_send.at[level, step - 1, part],
            recv_sem=swap_recv.at[level, step - 1, part],
            device_id=(target, strip),
            device_id_type=MESH,
        )

    def dispatch(level, part):
        radix = levels[level][0]
        for step in range(1, radix):
            swap(level, step, part, True).start()
        digit = partner(level, 1)[0]
        got[level][digit, part] = sent[level][digit, part]

    def fill(level, part, tile_of):
        radix, _, held, width = levels[level]
        per, count = piece_tiles(width)
        for j in range(radix):
            blocks = [q * radix + j for q in range(width // block)]
            if width >= LANES:
                each = LANES // block
                blocks = blocks[part * each:(part + 1) * each]
                for k in range(4):
                    sent[level][j, part, k] = place(
                        [
                            (tile_of(k, b * block // LANES), b * block % LANES, i * block, block)
                            for i, b in enumerate(blocks)
                        ],
                        lane,
                    )
            else:
                for c in range(count):
                    sent[level][j, part, c] = place(
                        [
                            (
                                tile_of(k, b * block // LANES), b * block % LANES,
                                (k - c * per) * width + i * block, block,
                            )
                            for k in range(c * per, min(4, (c + 1) * per))
                            for i, b in enumerate(blocks)
                        ],
                        lane,
                    )

    for c in range(stages):
        wait_halos(c, over_strip)
    lax.fori_loop(0, tiles, inner_field, 0)
    lax.fori_loop(0, tiles, inner_render, 0)

    for c in range(stages):
        wait_halos(c, over_depth)
        lax.fori_loop(starts[c], ends[c], outer_field, 0)
        lax.fori_loop(c * per_stage, (c + 1) * per_stage, outer_render, 0)
        fill(0, c, lambda k, t: picture[t, k])
        dispatch(0, c)

    current = None
    for level, (radix, _, held, width) in enumerate(levels):
        parts = max(1, width // LANES)
        if level > 0:
            for part in range(parts):
                fill(level, part, lambda k, t: current[t][k])
                dispatch(level, part)
        per, _ = piece_tiles(width)
        merged = []
        for part in range(parts):
            for step in range(1, radix):
                swap(level, step, part, False).wait_recv()

            def channel(j, k):
                tile = got[level][j, part, k // per]
                shift = -(k % per) * width % LANES
                return pltpu.roll(tile, shift, 1) if shift else tile

            value = [channel(0, k) for k in range(4)]
            for j in range(1, radix):
                value = over(value, [channel(j, k) for k in range(4)])
            merged.append(value)
        current = merged

    for k in range(4):
        out_ref[k] = current[0][k][:, :block]

    for c in range(stages):
        for index, (dz, ds) in enumerate(SIDES):
            @pl.when(there(dz, ds))
            def _(c=c, index=index):
                halo(c, index, True).wait_send()
    for level, (radix, _, _, width) in enumerate(levels):
        for part in range(max(1, width // LANES)):
            for step in range(1, radix):
                swap(level, step, part, True).wait_send()


def local(volume, extinction, color_map, light_direction):
    rows, slabs, columns = volume.shape
    groups, strips = lax.axis_size("depth"), lax.axis_size("strip")
    tiles, block = columns // LANES, columns // groups
    levels = plan(groups, columns)
    stages = max(1, levels[0][3] // LANES)
    f32 = jnp.float32
    buffers = []
    for radix, _, _, width in levels:
        parts = max(1, width // LANES)
        buffers.append(pltpu.VMEM((radix, parts, piece_tiles(width)[1] // parts, rows, LANES), f32))
    most = max(max(1, width // LANES) for _, _, _, width in levels)
    image = pl.pallas_call(
        functools.partial(kernel, groups, strips, rows, slabs, columns),
        out_shape=jax.ShapeDtypeStruct((4, rows, block), f32),
        in_specs=[pl.BlockSpec(memory_space=pl.ANY)] * 4,
        out_specs=pl.BlockSpec(memory_space=pltpu.VMEM),
        scratch_shapes=[
            pltpu.SMEM((1,), f32),
            pltpu.SMEM((2, 3), f32),
            pltpu.SMEM((3,), f32),
            pltpu.VMEM((tiles, rows * slabs, LANES), f32),
            pltpu.VMEM((tiles, slabs + 4, rows + 2 * EDGE, LANES), f32),
            pltpu.VMEM((tiles, slabs + 2, rows + 8, LANES), f32),
            pltpu.VMEM((tiles + 1, slabs, rows, LANES), f32),
            pltpu.VMEM((tiles + 1, slabs, rows, LANES), f32),
            pltpu.VMEM((tiles, 4, rows, LANES), f32),
            *buffers,
            *buffers,
            pltpu.SemaphoreType.DMA((tiles,)),
            pltpu.SemaphoreType.DMA((3,)),
            pltpu.SemaphoreType.DMA((stages, len(SIDES))),
            pltpu.SemaphoreType.DMA((stages, len(SIDES))),
            pltpu.SemaphoreType.DMA((len(levels), 3, most)),
            pltpu.SemaphoreType.DMA((len(levels), 3, most)),
        ],
        compiler_params=pltpu.CompilerParams(
            collective_id=0, has_side_effects=True, vmem_limit_bytes=60 * 1024 * 1024
        ),
    )(extinction, color_map.T, light_direction, volume.reshape(rows * slabs, columns))
    last = lax.broadcasted_iota(jnp.int32, image.shape, 0) == 3
    return jnp.where(last, 1.0 - image, image)


def solution(mesh):
    in_specs = (P("strip", "depth", None), P(), P(), P())
    out_specs = P(None, "strip", "depth")
    return jax.shard_map(local, mesh=mesh, in_specs=in_specs, out_specs=out_specs, check_vma=False)
```

```python
import functools
import math

import jax
import jax.numpy as jnp
from jax import lax
from jax.experimental import pallas as pl
from jax.experimental.pallas import tpu as pltpu
from jax.sharding import PartitionSpec as P

LANES = 128
EDGE = 8
MESH = pl.DeviceIdType.MESH
SIDES = [(dz, ds) for dz in (-1, 0, 1) for ds in (-1, 0, 1) if (dz, ds) != (0, 0)]


def radices_of(count):
    found = []
    while count > 1:
        radix = 4 if count % 4 == 0 else 2
        found.append(radix)
        count //= radix
    return found


def next_lane(here, after, lane):
    return pltpu.roll(jnp.where(lane == 0, after, here), LANES - 1, here.ndim - 1)


def previous_lane(here, before, lane):
    return pltpu.roll(jnp.where(lane == LANES - 1, before, here), 1, here.ndim - 1)


def place(parts, lane):
    result = None
    for tile, source, target, width in parts:
        shift = (target - source) % LANES
        moved = pltpu.roll(tile, shift, 1) if shift else tile
        if result is None:
            result = moved
        else:
            result = jnp.where((lane >= target) & (lane < target + width), moved, result)
    return result


def plan(groups, columns):
    levels, stride, held = [], 1, columns
    for radix in radices_of(groups):
        levels.append((radix, stride, held, held // radix))
        stride *= radix
        held //= radix
    return levels


def piece_tiles(width):
    if width >= LANES:
        return 1, 4 * (width // LANES)
    per = min(4, LANES // width)
    return per, -(-4 // per)


def kernel(groups, strips, rows, slabs, columns,
           ext_hbm, color_hbm, light_hbm, vol_ref, out_ref,
           ext_ref, color_ref, light_ref, vol, ext_field, smooth, ahead, behind, picture, *rest):
    levels = plan(groups, columns)
    sent = rest[:len(levels)]
    got = rest[len(levels):2 * len(levels)]
    load_sem, small_sem, halo_send, halo_recv, swap_send, swap_recv = rest[2 * len(levels):]
    tiles = columns // LANES
    block = columns // groups
    depth, strip = lax.axis_index("depth"), lax.axis_index("strip")
    lane = lax.broadcasted_iota(jnp.int32, (rows, LANES), 1)
    lane8 = lax.broadcasted_iota(jnp.int32, (8, LANES), 1)
    tall = rows + 8

    loads = [
        pltpu.make_async_copy(vol_ref.at[:, pl.ds(t * LANES, LANES)], vol.at[t], load_sem.at[t])
        for t in range(tiles)
    ]
    for load in loads:
        load.start()
    scalars = [
        pltpu.make_async_copy(source, target, small_sem.at[i])
        for i, (source, target) in enumerate(
            [(ext_hbm, ext_ref), (color_hbm, color_ref), (light_hbm, light_ref)])
    ]
    for scalar in scalars:
        scalar.start()

    def there(dz, ds):
        return (depth + dz >= 0) & (depth + dz < groups) & (strip + ds >= 0) & (strip + ds < strips)

    def partner(level, step):
        radix, stride, _, _ = levels[level]
        digit = depth // stride % radix
        other = (digit + step) % radix
        return digit, other, depth + (other - digit) * stride

    barrier = pltpu.get_barrier_semaphore()
    expected = 0
    for dz, ds in SIDES:
        expected = expected + jnp.where(there(dz, ds), 1, 0)

        @pl.when(there(dz, ds))
        def _(dz=dz, ds=ds):
            pl.semaphore_signal(barrier, inc=1, device_id=(depth + dz, strip + ds), device_id_type=MESH)

    for level, (radix, _, _, _) in enumerate(levels):
        for step in range(1, radix):
            pl.semaphore_signal(
                barrier, inc=1, device_id=(partner(level, step)[2], strip), device_id_type=MESH
            )
            expected = expected + 1

    @pl.when(depth == 0)
    def _():
        ext_field[:, 0:2] = jnp.zeros((tiles, 2, rows + 2 * EDGE, LANES), jnp.float32)

    @pl.when(depth == groups - 1)
    def _():
        ext_field[:, slabs + 2:] = jnp.zeros((tiles, 2, rows + 2 * EDGE, LANES), jnp.float32)

    @pl.when(strip == 0)
    def _():
        ext_field[:, :, 0:EDGE] = jnp.zeros((tiles, slabs + 4, EDGE, LANES), jnp.float32)

    @pl.when(strip == strips - 1)
    def _():
        ext_field[:, :, rows + EDGE:] = jnp.zeros((tiles, slabs + 4, EDGE, LANES), jnp.float32)

    ahead[tiles] = jnp.zeros((slabs, rows, LANES), jnp.float32)
    behind[0] = jnp.zeros((slabs, rows, LANES), jnp.float32)

    for load in loads:
        load.wait()

    first = levels[0]
    stages = max(1, first[3] // LANES)
    per_stage = tiles // stages
    ends = [min(tiles, (c + 1) * per_stage + 1) for c in range(stages)]
    starts = [0] + ends[:-1]

    def halo(c, index, sender):
        dz, ds = SIDES[index]
        span = pl.ds(starts[c], ends[c] - starts[c])
        z_from, z_to, z_count = {
            -1: (2, slabs + 2, 2), 0: (2, 2, slabs), 1: (slabs, 0, 2)}[dz]
        r_from, r_to, r_count = {
            -1: (EDGE, EDGE + rows, 2), 0: (EDGE, EDGE, rows), 1: (EDGE + rows - 2, EDGE - 2, 2)}[ds]
        sign = 1 if sender else -1
        return pltpu.make_async_remote_copy(
            src_ref=ext_field.at[span, pl.ds(z_from, z_count), pl.ds(r_from, r_count)],
            dst_ref=ext_field.at[span, pl.ds(z_to, z_count), pl.ds(r_to, r_count)],
            send_sem=halo_send.at[c, index],
            recv_sem=halo_recv.at[c, index],
            device_id=(depth + sign * dz, strip + sign * ds),
            device_id_type=MESH,
        )

    def blur_columns(z, carry):
        for h in range(rows // 8):
            cells = [vol[t, pl.ds(8 * h * slabs + z, 8, stride=slabs), :] for t in range(tiles)]
            nothing = jnp.zeros_like(cells[0])
            for t in range(tiles):
                before = cells[t - 1] if t > 0 else nothing
                after = cells[t + 1] if t < tiles - 1 else nothing
                ext_field[t, z + 2, EDGE + 8 * h:EDGE + 8 * h + 8] = (
                    next_lane(cells[t], after, lane8)
                    + previous_lane(cells[t], before, lane8)
                    + 2.0 * cells[t]
                )
        return carry

    def start_halos(chosen):
        for c in range(stages):
            for index in chosen:
                dz, ds = SIDES[index]

                @pl.when(there(dz, ds))
                def _(c=c, index=index):
                    halo(c, index, True).start()

    def wait_halos(c, chosen):
        for index in chosen:
            dz, ds = SIDES[index]

            @pl.when(there(-dz, -ds))
            def _(c=c, index=index):
                halo(c, index, False).wait_recv()

    over_depth = [i for i, (dz, _) in enumerate(SIDES) if dz != 0]
    over_strip = [i for i, (dz, _) in enumerate(SIDES) if dz == 0]
    lax.fori_loop(0, 2, blur_columns, 0)
    lax.fori_loop(slabs - 2, slabs, blur_columns, 0)
    pl.semaphore_wait(barrier, expected)
    start_halos(over_depth)
    lax.fori_loop(2, slabs - 2, blur_columns, 0)
    start_halos(over_strip)

    row = lax.broadcasted_iota(jnp.int32, (tall, LANES), 0)
    inside = ((row > 0) | (strip > 0)) & ((row != rows + 1) | (strip < strips - 1))
    scale = jnp.where(inside, 1.0 / 64.0, 0.0)
    scale_front = jnp.where(inside & (depth > 0), 1.0 / 64.0, 0.0)
    scale_back = jnp.where(inside & (depth < groups - 1), 1.0 / 64.0, 0.0)
    for scalar in scalars:
        scalar.wait()
    light = [light_ref[0] / 32.0, light_ref[1] / 32.0, light_ref[2] / 32.0]

    def smooth_slices(t, low, high):
        def over_rows(z):
            return (
                ext_field[t, z, EDGE - 2:EDGE - 2 + tall]
                + ext_field[t, z, EDGE:EDGE + tall]
                + 2.0 * ext_field[t, z, EDGE - 1:EDGE - 1 + tall]
            )

        one, two = over_rows(low), over_rows(low + 1)
        for z in range(low, high):
            three = over_rows(z + 2)
            weight = scale_front if z == 0 else scale_back if z == slabs + 1 else scale
            smooth[t, z] = jnp.where(weight > 0.0, (one + three + 2.0 * two) * weight, 0.0)
            one, two = two, three

    def gradients(t, low, high):
        def rows_of(z):
            under = smooth[t, z, 0:rows]
            middle = smooth[t, z, 1:rows + 1]
            over = smooth[t, z, 2:rows + 2]
            return under + over + 2.0 * middle, over - under

        one, two = rows_of(low), rows_of(low + 1)
        for z in range(low, high):
            three = rows_of(z + 2)
            across = (
                light[0] * (one[1] + three[1] + 2.0 * two[1])
                + light[1] * (three[0] - one[0])
            )
            along = light[2] * (one[0] + three[0] + 2.0 * two[0])
            ahead[t, z] = across + along
            behind[t + 1, z] = across - along
            one, two = two, three

    to_double = 2.0 / math.log(2.0)
    thinning = ext_ref[0] * (-1.0 / math.log(2.0))
    slope = [0.5 * color_ref[0, k] for k in range(3)]
    offset = [0.5 * color_ref[1, k] for k in range(3)]

    def render(t, low, high):
        density = jnp.zeros((rows, LANES), jnp.float32)
        passed = jnp.ones((rows, LANES), jnp.float32)
        total = jnp.zeros((rows, LANES), jnp.float32)
        tinted = [jnp.zeros((rows, LANES), jnp.float32) for _ in range(3)]
        for z in range(low, high):
            up, down = ahead[t, z], behind[t + 1, z]
            facing = (
                next_lane(up, ahead[t + 1, z], lane)
                + previous_lane(down, behind[t, z], lane)
                + (up + down)
            )
            stretch = 1.0 + facing * facing
            guess = pl.reciprocal(stretch, approx=True)
            inverse = guess * (2.0 - stretch * guess)
            field = smooth[t, z + 1, 1:rows + 1]
            density += jnp.log(1.0 + jnp.exp2(to_double * field))
            beyond = jnp.exp2(thinning * density)
            weight = (passed - beyond) * (1.0 - 0.7 * inverse)
            passed = beyond
            total += weight
            for k in range(3):
                tinted[k] += weight * jnp.tanh(slope[k] * field + offset[k])
        return [0.5 * (total + tinted[k]) for k in range(3)] + [passed]

    def over(front, back):
        return [front[k] + front[3] * back[k] for k in range(3)] + [front[3] * back[3]]

    inner = (2, max(2, slabs - 2))

    def inner_field(t, carry):
        smooth_slices(t, inner[0], inner[1] + 2)
        gradients(t, *inner)
        return carry

    def inner_render(t, carry):
        value = render(t, *inner)
        for k in range(4):
            picture[t, k] = value[k]
        return carry

    def outer_field(t, carry):
        smooth_slices(t, 0, inner[0])
        smooth_slices(t, inner[1] + 2, slabs + 2)
        gradients(t, 0, inner[0])
        gradients(t, inner[1], slabs)
        return carry

    def outer_render(t, carry):
        value = over(render(t, 0, inner[0]), [picture[t, k] for k in range(4)])
        value = over(value, render(t, inner[1], slabs))
        for k in range(4):
            picture[t, k] = value[k]
        return carry

    def swap(level, step, part, sender):
        digit, other, target = partner(level, step if sender else -step)
        source, slot = (other, digit) if sender else (digit, other)
        return pltpu.make_async_remote_copy(
            src_ref=sent[level].at[source, part],
            dst_ref=got[level].at[slot, part],
            send_sem=swap_send.at[level, step - 1, part],
            recv_sem=swap_recv.at[level, step - 1, part],
            device_id=(target, strip),
            device_id_type=MESH,
        )

    def dispatch(level, part):
        radix = levels[level][0]
        for step in range(1, radix):
            swap(level, step, part, True).start()
        digit = partner(level, 1)[0]
        got[level][digit, part] = sent[level][digit, part]

    def fill(level, part, tile_of):
        radix, _, held, width = levels[level]
        per, count = piece_tiles(width)
        for j in range(radix):
            blocks = [q * radix + j for q in range(width // block)]
            if width >= LANES:
                each = LANES // block
                blocks = blocks[part * each:(part + 1) * each]
                for k in range(4):
                    sent[level][j, part, k] = place(
                        [
                            (tile_of(k, b * block // LANES), b * block % LANES, i * block, block)
                            for i, b in enumerate(blocks)
                        ],
                        lane,
                    )
            else:
                for c in range(count):
                    sent[level][j, part, c] = place(
                        [
                            (
                                tile_of(k, b * block // LANES), b * block % LANES,
                                (k - c * per) * width + i * block, block,
                            )
                            for k in range(c * per, min(4, (c + 1) * per))
                            for i, b in enumerate(blocks)
                        ],
                        lane,
                    )

    for c in range(stages):
        wait_halos(c, over_strip)
    lax.fori_loop(0, tiles, inner_field, 0)
    lax.fori_loop(0, tiles, inner_render, 0)

    for c in range(stages):
        wait_halos(c, over_depth)
        lax.fori_loop(starts[c], ends[c], outer_field, 0)
        lax.fori_loop(c * per_stage, (c + 1) * per_stage, outer_render, 0)
        fill(0, c, lambda k, t: picture[t, k])
        dispatch(0, c)

    current = None
    for level, (radix, _, held, width) in enumerate(levels):
        parts = max(1, width // LANES)
        if level > 0:
            for part in range(parts):
                fill(level, part, lambda k, t: current[t][k])
                dispatch(level, part)
        per, _ = piece_tiles(width)
        merged = []
        for part in range(parts):
            for step in range(1, radix):
                swap(level, step, part, False).wait_recv()

            def channel(j, k):
                tile = got[level][j, part, k // per]
                shift = -(k % per) * width % LANES
                return pltpu.roll(tile, shift, 1) if shift else tile

            value = [channel(0, k) for k in range(4)]
            for j in range(1, radix):
                value = over(value, [channel(j, k) for k in range(4)])
            merged.append(value)
        current = merged

    for k in range(4):
        out_ref[k] = current[0][k][:, :block]

    for c in range(stages):
        for index, (dz, ds) in enumerate(SIDES):
            @pl.when(there(dz, ds))
            def _(c=c, index=index):
                halo(c, index, True).wait_send()
    for level, (radix, _, _, width) in enumerate(levels):
        for part in range(max(1, width // LANES)):
            for step in range(1, radix):
                swap(level, step, part, True).wait_send()


def local(volume, extinction, color_map, light_direction):
    rows, slabs, columns = volume.shape
    groups, strips = lax.axis_size("depth"), lax.axis_size("strip")
    tiles, block = columns // LANES, columns // groups
    levels = plan(groups, columns)
    stages = max(1, levels[0][3] // LANES)
    f32 = jnp.float32
    buffers = []
    for radix, _, _, width in levels:
        parts = max(1, width // LANES)
        buffers.append(pltpu.VMEM((radix, parts, piece_tiles(width)[1] // parts, rows, LANES), f32))
    most = max(max(1, width // LANES) for _, _, _, width in levels)
    image = pl.pallas_call(
        functools.partial(kernel, groups, strips, rows, slabs, columns),
        out_shape=jax.ShapeDtypeStruct((4, rows, block), f32),
        in_specs=[pl.BlockSpec(memory_space=pl.ANY)] * 4,
        out_specs=pl.BlockSpec(memory_space=pltpu.VMEM),
        scratch_shapes=[
            pltpu.SMEM((1,), f32),
            pltpu.SMEM((2, 3), f32),
            pltpu.SMEM((3,), f32),
            pltpu.VMEM((tiles, rows * slabs, LANES), f32),
            pltpu.VMEM((tiles, slabs + 4, rows + 2 * EDGE, LANES), f32),
            pltpu.VMEM((tiles, slabs + 2, rows + 8, LANES), f32),
            pltpu.VMEM((tiles + 1, slabs, rows, LANES), f32),
            pltpu.VMEM((tiles + 1, slabs, rows, LANES), f32),
            pltpu.VMEM((tiles, 4, rows, LANES), f32),
            *buffers,
            *buffers,
            pltpu.SemaphoreType.DMA((tiles,)),
            pltpu.SemaphoreType.DMA((3,)),
            pltpu.SemaphoreType.DMA((stages, len(SIDES))),
            pltpu.SemaphoreType.DMA((stages, len(SIDES))),
            pltpu.SemaphoreType.DMA((len(levels), 3, most)),
            pltpu.SemaphoreType.DMA((len(levels), 3, most)),
        ],
        compiler_params=pltpu.CompilerParams(
            collective_id=0, has_side_effects=True, vmem_limit_bytes=56 * 1024 * 1024
        ),
    )(extinction, color_map.T, light_direction, volume.reshape(rows * slabs, columns))
    last = lax.broadcasted_iota(jnp.int32, image.shape, 0) == 3
    return jnp.where(last, 1.0 - image, image)


def solution(mesh):
    in_specs = (P("strip", "depth", None), P(), P(), P())
    out_specs = P(None, "strip", "depth")
    return jax.shard_map(local, mesh=mesh, in_specs=in_specs, out_specs=out_specs, check_vma=False)
```

```python
import functools
import math

import jax
import jax.numpy as jnp
from jax import lax
from jax.experimental import pallas as pl
from jax.experimental.pallas import tpu as pltpu
from jax.sharding import PartitionSpec as P

LANES = 128
EDGE = 8
MESH = pl.DeviceIdType.MESH
SIDES = [(dz, ds) for dz in (-1, 0, 1) for ds in (-1, 0, 1) if (dz, ds) != (0, 0)]


def radices_of(count):
    found = []
    while count > 1:
        radix = 4 if count % 4 == 0 else 2
        found.append(radix)
        count //= radix
    return found


def next_lane(here, after, lane):
    return pltpu.roll(jnp.where(lane == 0, after, here), LANES - 1, here.ndim - 1)


def previous_lane(here, before, lane):
    return pltpu.roll(jnp.where(lane == LANES - 1, before, here), 1, here.ndim - 1)


def place(parts, lane):
    result = None
    for tile, source, target, width in parts:
        shift = (target - source) % LANES
        moved = pltpu.roll(tile, shift, 1) if shift else tile
        if result is None:
            result = moved
        else:
            result = jnp.where((lane >= target) & (lane < target + width), moved, result)
    return result


def plan(groups, columns):
    levels, stride, held = [], 1, columns
    for radix in radices_of(groups):
        levels.append((radix, stride, held, held // radix))
        stride *= radix
        held //= radix
    return levels


def piece_tiles(width):
    if width >= LANES:
        return 1, 4 * (width // LANES)
    per = min(4, LANES // width)
    return per, -(-4 // per)


def kernel(groups, strips, rows, slabs, columns,
           ext_hbm, color_hbm, light_hbm, vol_ref, out_ref,
           ext_ref, color_ref, light_ref, vol, ext_field, smooth, ahead, behind, picture, *rest):
    levels = plan(groups, columns)
    sent = rest[:len(levels)]
    got = rest[len(levels):2 * len(levels)]
    load_sem, small_sem, halo_send, halo_recv, swap_send, swap_recv = rest[2 * len(levels):]
    tiles = columns // LANES
    block = columns // groups
    depth, strip = lax.axis_index("depth"), lax.axis_index("strip")
    lane = lax.broadcasted_iota(jnp.int32, (rows, LANES), 1)
    lane8 = lax.broadcasted_iota(jnp.int32, (8, LANES), 1)
    tall = rows + 8

    loads = [
        pltpu.make_async_copy(vol_ref.at[:, pl.ds(t * LANES, LANES)], vol.at[t], load_sem.at[t])
        for t in range(tiles)
    ]
    for load in loads:
        load.start()
    scalars = [
        pltpu.make_async_copy(source, target, small_sem.at[i])
        for i, (source, target) in enumerate(
            [(ext_hbm, ext_ref), (color_hbm, color_ref), (light_hbm, light_ref)])
    ]
    for scalar in scalars:
        scalar.start()

    def there(dz, ds):
        return (depth + dz >= 0) & (depth + dz < groups) & (strip + ds >= 0) & (strip + ds < strips)

    def partner(level, step):
        radix, stride, _, _ = levels[level]
        digit = depth // stride % radix
        other = (digit + step) % radix
        return digit, other, depth + (other - digit) * stride

    barrier = pltpu.get_barrier_semaphore()
    expected = 0
    for dz, ds in SIDES:
        expected = expected + jnp.where(there(dz, ds), 1, 0)

        @pl.when(there(dz, ds))
        def _(dz=dz, ds=ds):
            pl.semaphore_signal(barrier, inc=1, device_id=(depth + dz, strip + ds), device_id_type=MESH)

    for level, (radix, _, _, _) in enumerate(levels):
        for step in range(1, radix):
            pl.semaphore_signal(
                barrier, inc=1, device_id=(partner(level, step)[2], strip), device_id_type=MESH
            )
            expected = expected + 1

    @pl.when(depth == 0)
    def _():
        ext_field[:, 0:2] = jnp.zeros((tiles, 2, rows + 2 * EDGE, LANES), jnp.float32)

    @pl.when(depth == groups - 1)
    def _():
        ext_field[:, slabs + 2:] = jnp.zeros((tiles, 2, rows + 2 * EDGE, LANES), jnp.float32)

    @pl.when(strip == 0)
    def _():
        ext_field[:, :, 0:EDGE] = jnp.zeros((tiles, slabs + 4, EDGE, LANES), jnp.float32)

    @pl.when(strip == strips - 1)
    def _():
        ext_field[:, :, rows + EDGE:] = jnp.zeros((tiles, slabs + 4, EDGE, LANES), jnp.float32)

    ahead[tiles] = jnp.zeros((slabs, rows, LANES), jnp.float32)
    behind[0] = jnp.zeros((slabs, rows, LANES), jnp.float32)

    for load in loads:
        load.wait()

    first = levels[0]
    stages = max(1, first[3] // LANES)
    per_stage = tiles // stages
    ends = [min(tiles, (c + 1) * per_stage + 1) for c in range(stages)]
    starts = [0] + ends[:-1]

    def halo(c, index, sender):
        dz, ds = SIDES[index]
        span = pl.ds(starts[c], ends[c] - starts[c])
        z_from, z_to, z_count = {
            -1: (2, slabs + 2, 2), 0: (2, 2, slabs), 1: (slabs, 0, 2)}[dz]
        r_from, r_to, r_count = {
            -1: (EDGE, EDGE + rows, 2), 0: (EDGE, EDGE, rows), 1: (EDGE + rows - 2, EDGE - 2, 2)}[ds]
        sign = 1 if sender else -1
        return pltpu.make_async_remote_copy(
            src_ref=ext_field.at[span, pl.ds(z_from, z_count), pl.ds(r_from, r_count)],
            dst_ref=ext_field.at[span, pl.ds(z_to, z_count), pl.ds(r_to, r_count)],
            send_sem=halo_send.at[c, index],
            recv_sem=halo_recv.at[c, index],
            device_id=(depth + sign * dz, strip + sign * ds),
            device_id_type=MESH,
        )

    def blur_columns(z, carry):
        for h in range(rows // 8):
            cells = [vol[t, pl.ds(8 * h * slabs + z, 8, stride=slabs), :] for t in range(tiles)]
            nothing = jnp.zeros_like(cells[0])
            for t in range(tiles):
                before = cells[t - 1] if t > 0 else nothing
                after = cells[t + 1] if t < tiles - 1 else nothing
                ext_field[t, z + 2, EDGE + 8 * h:EDGE + 8 * h + 8] = (
                    next_lane(cells[t], after, lane8)
                    + previous_lane(cells[t], before, lane8)
                    + 2.0 * cells[t]
                )
        return carry

    def start_halos(c, chosen):
        for index in chosen:
            dz, ds = SIDES[index]

            @pl.when(there(dz, ds))
            def _(c=c, index=index):
                halo(c, index, True).start()

    def leave_halos(c, chosen):
        for index in chosen:
            dz, ds = SIDES[index]

            @pl.when(there(dz, ds))
            def _(c=c, index=index):
                halo(c, index, True).wait_send()

    def wait_halos(c, chosen):
        for index in chosen:
            dz, ds = SIDES[index]

            @pl.when(there(-dz, -ds))
            def _(c=c, index=index):
                halo(c, index, False).wait_recv()

    over_depth = [i for i, (dz, _) in enumerate(SIDES) if dz != 0]
    over_strip = [i for i, (dz, _) in enumerate(SIDES) if dz == 0]
    lax.fori_loop(0, 2, blur_columns, 0)
    lax.fori_loop(slabs - 2, slabs, blur_columns, 0)
    pl.semaphore_wait(barrier, expected)
    start_halos(0, over_depth)
    lax.fori_loop(2, slabs - 2, blur_columns, 0)
    for c in range(stages):
        start_halos(c, over_strip)

    row = lax.broadcasted_iota(jnp.int32, (tall, LANES), 0)
    inside = ((row > 0) | (strip > 0)) & ((row != rows + 1) | (strip < strips - 1))
    scale = jnp.where(inside, 1.0 / 64.0, 0.0)
    scale_front = jnp.where(inside & (depth > 0), 1.0 / 64.0, 0.0)
    scale_back = jnp.where(inside & (depth < groups - 1), 1.0 / 64.0, 0.0)
    for scalar in scalars:
        scalar.wait()
    light = [light_ref[0] / 32.0, light_ref[1] / 32.0, light_ref[2] / 32.0]

    def smooth_slices(t, low, high):
        def over_rows(z):
            return (
                ext_field[t, z, EDGE - 2:EDGE - 2 + tall]
                + ext_field[t, z, EDGE:EDGE + tall]
                + 2.0 * ext_field[t, z, EDGE - 1:EDGE - 1 + tall]
            )

        one, two = over_rows(low), over_rows(low + 1)
        for z in range(low, high):
            three = over_rows(z + 2)
            weight = scale_front if z == 0 else scale_back if z == slabs + 1 else scale
            smooth[t, z] = jnp.where(weight > 0.0, (one + three + 2.0 * two) * weight, 0.0)
            one, two = two, three

    def gradients(t, low, high):
        def rows_of(z):
            under = smooth[t, z, 0:rows]
            middle = smooth[t, z, 1:rows + 1]
            over = smooth[t, z, 2:rows + 2]
            return under + over + 2.0 * middle, over - under

        one, two = rows_of(low), rows_of(low + 1)
        for z in range(low, high):
            three = rows_of(z + 2)
            across = (
                light[0] * (one[1] + three[1] + 2.0 * two[1])
                + light[1] * (three[0] - one[0])
            )
            along = light[2] * (one[0] + three[0] + 2.0 * two[0])
            ahead[t, z] = across + along
            behind[t + 1, z] = across - along
            one, two = two, three

    to_double = 2.0 / math.log(2.0)
    thinning = ext_ref[0] * (-1.0 / math.log(2.0))
    slope = [0.5 * color_ref[0, k] for k in range(3)]
    offset = [0.5 * color_ref[1, k] for k in range(3)]

    def render(t, low, high):
        density = jnp.zeros((rows, LANES), jnp.float32)
        passed = jnp.ones((rows, LANES), jnp.float32)
        total = jnp.zeros((rows, LANES), jnp.float32)
        tinted = [jnp.zeros((rows, LANES), jnp.float32) for _ in range(3)]
        for z in range(low, high):
            up, down = ahead[t, z], behind[t + 1, z]
            facing = (
                next_lane(up, ahead[t + 1, z], lane)
                + previous_lane(down, behind[t, z], lane)
                + (up + down)
            )
            stretch = 1.0 + facing * facing
            guess = pl.reciprocal(stretch, approx=True)
            inverse = guess * (2.0 - stretch * guess)
            field = smooth[t, z + 1, 1:rows + 1]
            density += jnp.log(1.0 + jnp.exp2(to_double * field))
            beyond = jnp.exp2(thinning * density)
            weight = (passed - beyond) * (1.0 - 0.7 * inverse)
            passed = beyond
            total += weight
            for k in range(3):
                tinted[k] += weight * jnp.tanh(slope[k] * field + offset[k])
        return [0.5 * (total + tinted[k]) for k in range(3)] + [passed]

    def over(front, back):
        return [front[k] + front[3] * back[k] for k in range(3)] + [front[3] * back[3]]

    inner = (2, max(2, slabs - 2))

    def inner_field(t, carry):
        smooth_slices(t, inner[0], inner[1] + 2)
        gradients(t, *inner)
        return carry

    def inner_render(t, carry):
        value = render(t, *inner)
        for k in range(4):
            picture[t, k] = value[k]
        return carry

    def outer_field(t, carry):
        smooth_slices(t, 0, inner[0])
        smooth_slices(t, inner[1] + 2, slabs + 2)
        gradients(t, 0, inner[0])
        gradients(t, inner[1], slabs)
        return carry

    def outer_render(t, carry):
        value = over(render(t, 0, inner[0]), [picture[t, k] for k in range(4)])
        value = over(value, render(t, inner[1], slabs))
        for k in range(4):
            picture[t, k] = value[k]
        return carry

    def swap(level, other, part, sender):
        radix, stride, _, _ = levels[level]
        digit = depth // stride % radix
        source, slot = (other, digit) if sender else (digit, other)
        return pltpu.make_async_remote_copy(
            src_ref=sent[level].at[source, part],
            dst_ref=got[level].at[slot, part],
            send_sem=swap_send.at[level, source, part],
            recv_sem=swap_recv.at[level, slot, part],
            device_id=(depth + (other - digit) * stride, strip),
            device_id_type=MESH,
        )

    def dispatch(level, j, part):
        radix, stride, _, _ = levels[level]
        digit = depth // stride % radix

        @pl.when(digit != j)
        def _():
            swap(level, j, part, True).start()

        @pl.when(digit == j)
        def _():
            got[level][j, part] = sent[level][j, part]

    def blocks_of(level, j, part):
        radix, _, _, width = levels[level]
        blocks = [q * radix + j for q in range(width // block)]
        if width >= LANES:
            each = LANES // block
            blocks = blocks[part * each:(part + 1) * each]
        return blocks

    def fill(level, j, part, tile_of):
        width = levels[level][3]
        per, _ = piece_tiles(width)
        count = -(-4 // per)
        for c in range(count):
            sent[level][j, part, c] = place(
                [
                    (
                        tile_of(k, b * block // LANES), b * block % LANES,
                        (k - c * per) * width % LANES + i * block, block,
                    )
                    for k in range(c * per, min(4, (c + 1) * per))
                    for i, b in enumerate(blocks_of(level, j, part))
                ],
                lane,
            )

    for c in range(stages):
        wait_halos(c, over_strip)
    lax.fori_loop(0, tiles, inner_field, 0)
    lax.fori_loop(0, tiles, inner_render, 0)

    for c in range(stages):
        leave_halos(c, over_depth)
        if c + 1 < stages:
            start_halos(c + 1, over_depth)
        wait_halos(c, over_depth)
        lax.fori_loop(starts[c], ends[c], outer_field, 0)
        lax.fori_loop(c * per_stage, (c + 1) * per_stage, outer_render, 0)
        for j in range(first[0]):
            fill(0, j, c, lambda k, t: picture[t, k])
            dispatch(0, j, c)

    current = []
    for level, (radix, stride, held, width) in enumerate(levels):
        per, _ = piece_tiles(width)
        digit = depth // stride % radix
        current, gone = [], set()
        for part in range(max(1, width // LANES)):
            for step in range(1, radix):
                swap(level, (digit + step) % radix, part, False).wait_recv()

            def channel(j, k):
                tile = got[level][j, part, k // per]
                shift = -(k % per) * width % LANES
                return pltpu.roll(tile, shift, 1) if shift else tile

            value = [channel(0, k) for k in range(4)]
            for j in range(1, radix):
                value = over(value, [channel(j, k) for k in range(4)])
            current.append(value)
            if level + 1 < len(levels):
                following, _, _, narrower = levels[level + 1]
                for j in range(following):
                    for later in range(max(1, narrower // LANES)):
                        needed = {b * block // LANES for b in blocks_of(level + 1, j, later)}
                        if (j, later) not in gone and max(needed) <= part:
                            gone.add((j, later))
                            fill(level + 1, j, later, lambda k, t: current[t][k])
                            dispatch(level + 1, j, later)

    for k in range(4):
        out_ref[k] = current[0][k][:, :block]

    for c in range(stages):
        leave_halos(c, over_strip)
    for level, (radix, stride, _, width) in enumerate(levels):
        digit = depth // stride % radix
        for part in range(max(1, width // LANES)):
            for step in range(1, radix):
                swap(level, (digit + step) % radix, part, True).wait_send()


def local(volume, extinction, color_map, light_direction):
    rows, slabs, columns = volume.shape
    groups, strips = lax.axis_size("depth"), lax.axis_size("strip")
    tiles, block = columns // LANES, columns // groups
    levels = plan(groups, columns)
    stages = max(1, levels[0][3] // LANES)
    f32 = jnp.float32
    buffers = []
    for radix, _, _, width in levels:
        parts = max(1, width // LANES)
        buffers.append(pltpu.VMEM((radix, parts, piece_tiles(width)[1] // parts, rows, LANES), f32))
    most = max(max(1, width // LANES) for _, _, _, width in levels)
    image = pl.pallas_call(
        functools.partial(kernel, groups, strips, rows, slabs, columns),
        out_shape=jax.ShapeDtypeStruct((4, rows, block), f32),
        in_specs=[pl.BlockSpec(memory_space=pl.ANY)] * 4,
        out_specs=pl.BlockSpec(memory_space=pltpu.VMEM),
        scratch_shapes=[
            pltpu.SMEM((1,), f32),
            pltpu.SMEM((2, 3), f32),
            pltpu.SMEM((3,), f32),
            pltpu.VMEM((tiles, rows * slabs, LANES), f32),
            pltpu.VMEM((tiles, slabs + 4, rows + 2 * EDGE, LANES), f32),
            pltpu.VMEM((tiles, slabs + 2, rows + 8, LANES), f32),
            pltpu.VMEM((tiles + 1, slabs, rows, LANES), f32),
            pltpu.VMEM((tiles + 1, slabs, rows, LANES), f32),
            pltpu.VMEM((tiles, 4, rows, LANES), f32),
            *buffers,
            *buffers,
            pltpu.SemaphoreType.DMA((tiles,)),
            pltpu.SemaphoreType.DMA((3,)),
            pltpu.SemaphoreType.DMA((stages, len(SIDES))),
            pltpu.SemaphoreType.DMA((stages, len(SIDES))),
            pltpu.SemaphoreType.DMA((len(levels), 4, most)),
            pltpu.SemaphoreType.DMA((len(levels), 4, most)),
        ],
        compiler_params=pltpu.CompilerParams(
            collective_id=0, has_side_effects=True, vmem_limit_bytes=56 * 1024 * 1024
        ),
    )(extinction, color_map.T, light_direction, volume.reshape(rows * slabs, columns))
    last = lax.broadcasted_iota(jnp.int32, image.shape, 0) == 3
    return jnp.where(last, 1.0 - image, image)


def solution(mesh):
    in_specs = (P("strip", "depth", None), P(), P(), P())
    out_specs = P(None, "strip", "depth")
    return jax.shard_map(local, mesh=mesh, in_specs=in_specs, out_specs=out_specs, check_vma=False)
```

```python
import functools
import math

import jax
import jax.numpy as jnp
from jax import lax
from jax.experimental import pallas as pl
from jax.experimental.pallas import tpu as pltpu
from jax.sharding import PartitionSpec as P

LANES = 128
EDGE = 8
MESH = pl.DeviceIdType.MESH
SIDES = [(dz, ds) for dz in (-1, 0, 1) for ds in (-1, 0, 1) if (dz, ds) != (0, 0)]


def radices_of(count):
    found = []
    while count > 1:
        radix = 4 if count % 4 == 0 else 2
        found.append(radix)
        count //= radix
    return found


def next_lane(here, after, lane):
    return pltpu.roll(jnp.where(lane == 0, after, here), LANES - 1, here.ndim - 1)


def previous_lane(here, before, lane):
    return pltpu.roll(jnp.where(lane == LANES - 1, before, here), 1, here.ndim - 1)


def place(parts, lane):
    result = None
    for tile, source, target, width in parts:
        shift = (target - source) % LANES
        moved = pltpu.roll(tile, shift, 1) if shift else tile
        if result is None:
            result = moved
        else:
            result = jnp.where((lane >= target) & (lane < target + width), moved, result)
    return result


def stages_of(groups, columns):
    return max(1, min(columns // LANES // 2, columns // (radices_of(groups)[0] * columns // groups)))


def plan(groups, columns):
    levels, stride, held = [], 1, columns
    for radix in radices_of(groups):
        width = held // radix
        part = min(width, LANES)
        if not levels:
            part = min(part, width // stages_of(groups, columns))
        levels.append((radix, stride, width, part, width // part))
        stride *= radix
        held = width
    return levels


def packing(part):
    per = min(4, LANES // part)
    return per, -(-4 // per)


def kernel(groups, strips, rows, slabs, columns,
           ext_hbm, color_hbm, light_hbm, vol_ref, out_ref,
           ext_ref, color_ref, light_ref, vol, ext_field, smooth, ahead, behind, picture, *rest):
    levels = plan(groups, columns)
    sent = rest[:len(levels)]
    got = rest[len(levels):2 * len(levels)]
    load_sem, small_sem, halo_send, halo_recv, swap_send, swap_recv = rest[2 * len(levels):]
    tiles = columns // LANES
    block = columns // groups
    depth, strip = lax.axis_index("depth"), lax.axis_index("strip")
    lane = lax.broadcasted_iota(jnp.int32, (rows, LANES), 1)
    lane8 = lax.broadcasted_iota(jnp.int32, (8, LANES), 1)
    tall = rows + 8

    loads = [
        pltpu.make_async_copy(vol_ref.at[:, pl.ds(t * LANES, LANES)], vol.at[t], load_sem.at[t])
        for t in range(tiles)
    ]
    for load in loads:
        load.start()
    scalars = [
        pltpu.make_async_copy(source, target, small_sem.at[i])
        for i, (source, target) in enumerate(
            [(ext_hbm, ext_ref), (color_hbm, color_ref), (light_hbm, light_ref)])
    ]
    for scalar in scalars:
        scalar.start()

    def there(dz, ds):
        return (depth + dz >= 0) & (depth + dz < groups) & (strip + ds >= 0) & (strip + ds < strips)

    barrier = pltpu.get_barrier_semaphore()
    expected = 0
    for dz, ds in SIDES:
        expected = expected + jnp.where(there(dz, ds), 1, 0)

        @pl.when(there(dz, ds))
        def _(dz=dz, ds=ds):
            pl.semaphore_signal(barrier, inc=1, device_id=(depth + dz, strip + ds), device_id_type=MESH)

    for radix, stride, _, _, _ in levels:
        digit = depth // stride % radix
        for step in range(1, radix):
            other = depth + ((digit + step) % radix - digit) * stride
            pl.semaphore_signal(barrier, inc=1, device_id=(other, strip), device_id_type=MESH)
            expected = expected + 1

    @pl.when(depth == 0)
    def _():
        ext_field[:, 0:2] = jnp.zeros((tiles, 2, rows + 2 * EDGE, LANES), jnp.float32)

    @pl.when(depth == groups - 1)
    def _():
        ext_field[:, slabs + 2:] = jnp.zeros((tiles, 2, rows + 2 * EDGE, LANES), jnp.float32)

    @pl.when(strip == 0)
    def _():
        ext_field[:, :, 0:EDGE] = jnp.zeros((tiles, slabs + 4, EDGE, LANES), jnp.float32)

    @pl.when(strip == strips - 1)
    def _():
        ext_field[:, :, rows + EDGE:] = jnp.zeros((tiles, slabs + 4, EDGE, LANES), jnp.float32)

    ahead[tiles] = jnp.zeros((slabs, rows, LANES), jnp.float32)
    behind[0] = jnp.zeros((slabs, rows, LANES), jnp.float32)

    for load in loads:
        load.wait()

    first = levels[0]
    stages = first[4]
    per_stage = tiles // stages
    ends = [min(tiles, (c + 1) * per_stage + 1) for c in range(stages)]
    starts = [0] + ends[:-1]

    def halo(c, index, sender):
        dz, ds = SIDES[index]
        span = pl.ds(starts[c], ends[c] - starts[c])
        z_from, z_to, z_count = {
            -1: (2, slabs + 2, 2), 0: (2, 2, slabs), 1: (slabs, 0, 2)}[dz]
        r_from, r_to, r_count = {
            -1: (EDGE, EDGE + rows, 2), 0: (EDGE, EDGE, rows), 1: (EDGE + rows - 2, EDGE - 2, 2)}[ds]
        sign = 1 if sender else -1
        return pltpu.make_async_remote_copy(
            src_ref=ext_field.at[span, pl.ds(z_from, z_count), pl.ds(r_from, r_count)],
            dst_ref=ext_field.at[span, pl.ds(z_to, z_count), pl.ds(r_to, r_count)],
            send_sem=halo_send.at[c, index],
            recv_sem=halo_recv.at[c, index],
            device_id=(depth + sign * dz, strip + sign * ds),
            device_id_type=MESH,
        )

    def blur_columns(z, carry):
        for h in range(rows // 8):
            cells = [vol[t, pl.ds(8 * h * slabs + z, 8, stride=slabs), :] for t in range(tiles)]
            nothing = jnp.zeros_like(cells[0])
            for t in range(tiles):
                before = cells[t - 1] if t > 0 else nothing
                after = cells[t + 1] if t < tiles - 1 else nothing
                ext_field[t, z + 2, EDGE + 8 * h:EDGE + 8 * h + 8] = (
                    next_lane(cells[t], after, lane8)
                    + previous_lane(cells[t], before, lane8)
                    + 2.0 * cells[t]
                )
        return carry

    def start_halos(c, chosen):
        for index in chosen:
            dz, ds = SIDES[index]

            @pl.when(there(dz, ds))
            def _(c=c, index=index):
                halo(c, index, True).start()

    def leave_halos(c, chosen):
        for index in chosen:
            dz, ds = SIDES[index]

            @pl.when(there(dz, ds))
            def _(c=c, index=index):
                halo(c, index, True).wait_send()

    def wait_halos(c, chosen):
        for index in chosen:
            dz, ds = SIDES[index]

            @pl.when(there(-dz, -ds))
            def _(c=c, index=index):
                halo(c, index, False).wait_recv()

    over_depth = [i for i, (dz, _) in enumerate(SIDES) if dz != 0]
    over_strip = [i for i, (dz, _) in enumerate(SIDES) if dz == 0]
    lax.fori_loop(0, 2, blur_columns, 0)
    lax.fori_loop(slabs - 2, slabs, blur_columns, 0)
    pl.semaphore_wait(barrier, expected)
    start_halos(0, over_depth)
    lax.fori_loop(2, slabs - 2, blur_columns, 0)
    for c in range(stages):
        start_halos(c, over_strip)

    row = lax.broadcasted_iota(jnp.int32, (tall, LANES), 0)
    inside = ((row > 0) | (strip > 0)) & ((row != rows + 1) | (strip < strips - 1))
    scale = jnp.where(inside, 1.0 / 64.0, 0.0)
    scale_front = jnp.where(inside & (depth > 0), 1.0 / 64.0, 0.0)
    scale_back = jnp.where(inside & (depth < groups - 1), 1.0 / 64.0, 0.0)
    for scalar in scalars:
        scalar.wait()
    light = [light_ref[0] / 32.0, light_ref[1] / 32.0, light_ref[2] / 32.0]

    def smooth_slices(t, low, high):
        def over_rows(z):
            return (
                ext_field[t, z, EDGE - 2:EDGE - 2 + tall]
                + ext_field[t, z, EDGE:EDGE + tall]
                + 2.0 * ext_field[t, z, EDGE - 1:EDGE - 1 + tall]
            )

        one, two = over_rows(low), over_rows(low + 1)
        for z in range(low, high):
            three = over_rows(z + 2)
            weight = scale_front if z == 0 else scale_back if z == slabs + 1 else scale
            smooth[t, z] = jnp.where(weight > 0.0, (one + three + 2.0 * two) * weight, 0.0)
            one, two = two, three

    def gradients(t, low, high):
        def rows_of(z):
            under = smooth[t, z, 0:rows]
            middle = smooth[t, z, 1:rows + 1]
            over = smooth[t, z, 2:rows + 2]
            return under + over + 2.0 * middle, over - under

        one, two = rows_of(low), rows_of(low + 1)
        for z in range(low, high):
            three = rows_of(z + 2)
            across = (
                light[0] * (one[1] + three[1] + 2.0 * two[1])
                + light[1] * (three[0] - one[0])
            )
            along = light[2] * (one[0] + three[0] + 2.0 * two[0])
            ahead[t, z] = across + along
            behind[t + 1, z] = across - along
            one, two = two, three

    to_double = 2.0 / math.log(2.0)
    thinning = ext_ref[0] * (-1.0 / math.log(2.0))
    slope = [0.5 * color_ref[0, k] for k in range(3)]
    offset = [0.5 * color_ref[1, k] for k in range(3)]

    def render(t, low, high):
        density = jnp.zeros((rows, LANES), jnp.float32)
        passed = jnp.ones((rows, LANES), jnp.float32)
        total = jnp.zeros((rows, LANES), jnp.float32)
        tinted = [jnp.zeros((rows, LANES), jnp.float32) for _ in range(3)]
        for z in range(low, high):
            up, down = ahead[t, z], behind[t + 1, z]
            facing = (
                next_lane(up, ahead[t + 1, z], lane)
                + previous_lane(down, behind[t, z], lane)
                + (up + down)
            )
            stretch = 1.0 + facing * facing
            guess = pl.reciprocal(stretch, approx=True)
            inverse = guess * (2.0 - stretch * guess)
            field = smooth[t, z + 1, 1:rows + 1]
            density += jnp.log(1.0 + jnp.exp2(to_double * field))
            beyond = jnp.exp2(thinning * density)
            weight = (passed - beyond) * (1.0 - 0.7 * inverse)
            passed = beyond
            total += weight
            for k in range(3):
                tinted[k] += weight * jnp.tanh(slope[k] * field + offset[k])
        return [0.5 * (total + tinted[k]) for k in range(3)] + [passed]

    def over(front, back):
        return [front[k] + front[3] * back[k] for k in range(3)] + [front[3] * back[3]]

    inner = (2, max(2, slabs - 2))

    def inner_field(t, carry):
        smooth_slices(t, inner[0], inner[1] + 2)
        gradients(t, *inner)
        return carry

    def inner_render(t, carry):
        value = render(t, *inner)
        for k in range(4):
            picture[t, k] = value[k]
        return carry

    def outer_field(t, carry):
        smooth_slices(t, 0, inner[0])
        smooth_slices(t, inner[1] + 2, slabs + 2)
        gradients(t, 0, inner[0])
        gradients(t, inner[1], slabs)
        return carry

    def outer_render(t, carry):
        value = over(render(t, 0, inner[0]), [picture[t, k] for k in range(4)])
        value = over(value, render(t, inner[1], slabs))
        for k in range(4):
            picture[t, k] = value[k]
        return carry

    def swap(level, other, part, sender):
        radix, stride = levels[level][:2]
        digit = depth // stride % radix
        source, slot = (other, digit) if sender else (digit, other)
        return pltpu.make_async_remote_copy(
            src_ref=sent[level].at[source, part],
            dst_ref=got[level].at[slot, part],
            send_sem=swap_send.at[level, source, part],
            recv_sem=swap_recv.at[level, slot, part],
            device_id=(depth + (other - digit) * stride, strip),
            device_id_type=MESH,
        )

    def dispatch(level, j, part):
        radix, stride = levels[level][:2]
        digit = depth // stride % radix

        @pl.when(digit != j)
        def _():
            swap(level, j, part, True).start()

        @pl.when(digit == j)
        def _():
            got[level][j, part] = sent[level][j, part]

    def blocks_of(level, j, part):
        radix, _, _, width, _ = levels[level]
        each = width // block
        return [q * radix + j for q in range(part * each, (part + 1) * each)]

    def fill(level, j, part, tile_of, span):
        width = levels[level][3]
        per, count = packing(width)
        for c in range(count):
            sent[level][j, part, c] = place(
                [
                    (
                        tile_of(k, b * block // span), b * block % span,
                        (k - c * per) * width + i * block, block,
                    )
                    for k in range(c * per, min(4, (c + 1) * per))
                    for i, b in enumerate(blocks_of(level, j, part))
                ],
                lane,
            )

    for c in range(stages):
        wait_halos(c, over_strip)
    lax.fori_loop(0, tiles, inner_field, 0)
    lax.fori_loop(0, tiles, inner_render, 0)

    for c in range(stages):
        leave_halos(c, over_depth)
        if c + 1 < stages:
            start_halos(c + 1, over_depth)
        wait_halos(c, over_depth)
        lax.fori_loop(starts[c], ends[c], outer_field, 0)
        lax.fori_loop(c * per_stage, (c + 1) * per_stage, outer_render, 0)
        for j in range(first[0]):
            fill(0, j, c, lambda k, t: picture[t, k], LANES)
            dispatch(0, j, c)

    current = []
    for level, (radix, stride, _, width, parts) in enumerate(levels):
        per, _ = packing(width)
        digit = depth // stride % radix
        current, gone = [], set()
        for part in range(parts):
            for step in range(1, radix):
                swap(level, (digit + step) % radix, part, False).wait_recv()

            def channel(j, k):
                tile = got[level][j, part, k // per]
                shift = -(k % per) * width % LANES
                return pltpu.roll(tile, shift, 1) if shift else tile

            value = [channel(0, k) for k in range(4)]
            for j in range(1, radix):
                value = over(value, [channel(j, k) for k in range(4)])
            current.append(value)
            if level + 1 < len(levels):
                for j in range(levels[level + 1][0]):
                    for later in range(levels[level + 1][4]):
                        needed = [b * block // width for b in blocks_of(level + 1, j, later)]
                        if (j, later) not in gone and max(needed) <= part:
                            gone.add((j, later))
                            fill(level + 1, j, later, lambda k, t: current[t][k], width)
                            dispatch(level + 1, j, later)

    for k in range(4):
        out_ref[k] = current[0][k][:, :block]

    for c in range(stages):
        leave_halos(c, over_strip)
    for level, (radix, stride, _, _, parts) in enumerate(levels):
        digit = depth // stride % radix
        for part in range(parts):
            for step in range(1, radix):
                swap(level, (digit + step) % radix, part, True).wait_send()


def local(volume, extinction, color_map, light_direction):
    rows, slabs, columns = volume.shape
    groups, strips = lax.axis_size("depth"), lax.axis_size("strip")
    tiles, block = columns // LANES, columns // groups
    levels = plan(groups, columns)
    stages = levels[0][4]
    f32 = jnp.float32
    buffers = []
    for radix, _, _, width, parts in levels:
        buffers.append(pltpu.VMEM((radix, parts, packing(width)[1], rows, LANES), f32))
    most = max(level[4] for level in levels)
    image = pl.pallas_call(
        functools.partial(kernel, groups, strips, rows, slabs, columns),
        out_shape=jax.ShapeDtypeStruct((4, rows, block), f32),
        in_specs=[pl.BlockSpec(memory_space=pl.ANY)] * 4,
        out_specs=pl.BlockSpec(memory_space=pltpu.VMEM),
        scratch_shapes=[
            pltpu.SMEM((1,), f32),
            pltpu.SMEM((2, 3), f32),
            pltpu.SMEM((3,), f32),
            pltpu.VMEM((tiles, rows * slabs, LANES), f32),
            pltpu.VMEM((tiles, slabs + 4, rows + 2 * EDGE, LANES), f32),
            pltpu.VMEM((tiles, slabs + 2, rows + 8, LANES), f32),
            pltpu.VMEM((tiles + 1, slabs, rows, LANES), f32),
            pltpu.VMEM((tiles + 1, slabs, rows, LANES), f32),
            pltpu.VMEM((tiles, 4, rows, LANES), f32),
            *buffers,
            *buffers,
            pltpu.SemaphoreType.DMA((tiles,)),
            pltpu.SemaphoreType.DMA((3,)),
            pltpu.SemaphoreType.DMA((stages, len(SIDES))),
            pltpu.SemaphoreType.DMA((stages, len(SIDES))),
            pltpu.SemaphoreType.DMA((len(levels), 4, most)),
            pltpu.SemaphoreType.DMA((len(levels), 4, most)),
        ],
        compiler_params=pltpu.CompilerParams(
            collective_id=0, has_side_effects=True, vmem_limit_bytes=56 * 1024 * 1024
        ),
    )(extinction, color_map.T, light_direction, volume.reshape(rows * slabs, columns))
    last = lax.broadcasted_iota(jnp.int32, image.shape, 0) == 3
    return jnp.where(last, 1.0 - image, image)


def solution(mesh):
    in_specs = (P("strip", "depth", None), P(), P(), P())
    out_specs = P(None, "strip", "depth")
    return jax.shard_map(local, mesh=mesh, in_specs=in_specs, out_specs=out_specs, check_vma=False)
```

```python
import functools
import math

import jax
import jax.numpy as jnp
from jax import lax
from jax.experimental import pallas as pl
from jax.experimental.pallas import tpu as pltpu
from jax.sharding import PartitionSpec as P

LANES = 128
EDGE = 8
MESH = pl.DeviceIdType.MESH
SIDES = [(dz, ds) for dz in (-1, 0, 1) for ds in (-1, 0, 1) if (dz, ds) != (0, 0)]


def radices_of(count):
    found = []
    while count > 1:
        radix = 4 if count % 4 == 0 else 2
        found.append(radix)
        count //= radix
    return found


def next_lane(here, after, lane):
    return pltpu.roll(jnp.where(lane == 0, after, here), LANES - 1, here.ndim - 1)


def previous_lane(here, before, lane):
    return pltpu.roll(jnp.where(lane == LANES - 1, before, here), 1, here.ndim - 1)


def place(parts, lane):
    result = None
    for tile, source, target, width in parts:
        shift = (target - source) % LANES
        moved = pltpu.roll(tile, shift, 1) if shift else tile
        if result is None:
            result = moved
        else:
            result = jnp.where((lane >= target) & (lane < target + width), moved, result)
    return result


def stages_of(groups, columns):
    return max(1, min(columns // LANES // 4, columns // (radices_of(groups)[0] * columns // groups)))


def plan(groups, columns):
    levels, stride, held = [], 1, columns
    for radix in radices_of(groups):
        width = held // radix
        part = min(width, LANES)
        if not levels:
            part = min(part, width // stages_of(groups, columns))
        levels.append((radix, stride, width, part, width // part))
        stride *= radix
        held = width
    return levels


def packing(part):
    per = min(4, LANES // part)
    return per, -(-4 // per)


def kernel(groups, strips, rows, slabs, columns,
           ext_hbm, color_hbm, light_hbm, vol_ref, out_ref,
           ext_ref, color_ref, light_ref, vol, ext_field, smooth, ahead, behind, picture, *rest):
    levels = plan(groups, columns)
    sent = rest[:len(levels)]
    got = rest[len(levels):2 * len(levels)]
    load_sem, small_sem, halo_send, halo_recv, swap_send, swap_recv = rest[2 * len(levels):]
    tiles = columns // LANES
    block = columns // groups
    depth, strip = lax.axis_index("depth"), lax.axis_index("strip")
    lane = lax.broadcasted_iota(jnp.int32, (rows, LANES), 1)
    lane8 = lax.broadcasted_iota(jnp.int32, (8, LANES), 1)
    tall = rows + 8

    loads = [
        pltpu.make_async_copy(vol_ref.at[:, pl.ds(t * LANES, LANES)], vol.at[t], load_sem.at[t])
        for t in range(tiles)
    ]
    for load in loads:
        load.start()
    scalars = [
        pltpu.make_async_copy(source, target, small_sem.at[i])
        for i, (source, target) in enumerate(
            [(ext_hbm, ext_ref), (color_hbm, color_ref), (light_hbm, light_ref)])
    ]
    for scalar in scalars:
        scalar.start()

    def there(dz, ds):
        return (depth + dz >= 0) & (depth + dz < groups) & (strip + ds >= 0) & (strip + ds < strips)

    barrier = pltpu.get_barrier_semaphore()
    expected = 0
    for dz, ds in SIDES:
        expected = expected + jnp.where(there(dz, ds), 1, 0)

        @pl.when(there(dz, ds))
        def _(dz=dz, ds=ds):
            pl.semaphore_signal(barrier, inc=1, device_id=(depth + dz, strip + ds), device_id_type=MESH)

    for radix, stride, _, _, _ in levels:
        digit = depth // stride % radix
        for step in range(1, radix):
            other = depth + ((digit + step) % radix - digit) * stride
            pl.semaphore_signal(barrier, inc=1, device_id=(other, strip), device_id_type=MESH)
            expected = expected + 1

    @pl.when(depth == 0)
    def _():
        ext_field[:, 0:2] = jnp.zeros((tiles, 2, rows + 2 * EDGE, LANES), jnp.float32)

    @pl.when(depth == groups - 1)
    def _():
        ext_field[:, slabs + 2:] = jnp.zeros((tiles, 2, rows + 2 * EDGE, LANES), jnp.float32)

    @pl.when(strip == 0)
    def _():
        ext_field[:, :, 0:EDGE] = jnp.zeros((tiles, slabs + 4, EDGE, LANES), jnp.float32)

    @pl.when(strip == strips - 1)
    def _():
        ext_field[:, :, rows + EDGE:] = jnp.zeros((tiles, slabs + 4, EDGE, LANES), jnp.float32)

    ahead[tiles] = jnp.zeros((slabs, rows, LANES), jnp.float32)
    behind[0] = jnp.zeros((slabs, rows, LANES), jnp.float32)

    for load in loads:
        load.wait()

    first = levels[0]
    stages = first[4]
    per_stage = tiles // stages
    ends = [min(tiles, (c + 1) * per_stage + 1) for c in range(stages)]
    starts = [0] + ends[:-1]
    spans = [(0, ends[0] // 2), (ends[0] // 2, ends[0])] + list(zip(starts[1:], ends[1:]))

    def halo(c, index, sender):
        dz, ds = SIDES[index]
        low, high = spans[c] if dz != 0 else (0, tiles)
        span = pl.ds(low, high - low)
        z_from, z_to, z_count = {
            -1: (2, slabs + 2, 2), 0: (2, 2, slabs), 1: (slabs, 0, 2)}[dz]
        r_from, r_to, r_count = {
            -1: (EDGE, EDGE + rows, 2), 0: (EDGE, EDGE, rows), 1: (EDGE + rows - 2, EDGE - 2, 2)}[ds]
        sign = 1 if sender else -1
        return pltpu.make_async_remote_copy(
            src_ref=ext_field.at[span, pl.ds(z_from, z_count), pl.ds(r_from, r_count)],
            dst_ref=ext_field.at[span, pl.ds(z_to, z_count), pl.ds(r_to, r_count)],
            send_sem=halo_send.at[c, index],
            recv_sem=halo_recv.at[c, index],
            device_id=(depth + sign * dz, strip + sign * ds),
            device_id_type=MESH,
        )

    def blur_columns(z, carry):
        for h in range(rows // 8):
            cells = [vol[t, pl.ds(8 * h * slabs + z, 8, stride=slabs), :] for t in range(tiles)]
            nothing = jnp.zeros_like(cells[0])
            for t in range(tiles):
                before = cells[t - 1] if t > 0 else nothing
                after = cells[t + 1] if t < tiles - 1 else nothing
                ext_field[t, z + 2, EDGE + 8 * h:EDGE + 8 * h + 8] = (
                    next_lane(cells[t], after, lane8)
                    + previous_lane(cells[t], before, lane8)
                    + 2.0 * cells[t]
                )
        return carry

    def start_halos(c, chosen):
        for index in chosen:
            dz, ds = SIDES[index]

            @pl.when(there(dz, ds))
            def _(c=c, index=index):
                halo(c, index, True).start()

    def leave_halos(c, chosen):
        for index in chosen:
            dz, ds = SIDES[index]

            @pl.when(there(dz, ds))
            def _(c=c, index=index):
                halo(c, index, True).wait_send()

    def wait_halos(c, chosen):
        for index in chosen:
            dz, ds = SIDES[index]

            @pl.when(there(-dz, -ds))
            def _(c=c, index=index):
                halo(c, index, False).wait_recv()

    over_depth = [i for i, (dz, _) in enumerate(SIDES) if dz != 0]
    over_strip = [i for i, (dz, _) in enumerate(SIDES) if dz == 0]
    lax.fori_loop(0, 2, blur_columns, 0)
    lax.fori_loop(slabs - 2, slabs, blur_columns, 0)
    pl.semaphore_wait(barrier, expected)
    start_halos(0, over_depth)
    start_halos(1, over_depth)
    lax.fori_loop(2, slabs - 2, blur_columns, 0)
    start_halos(0, over_strip)

    row = lax.broadcasted_iota(jnp.int32, (tall, LANES), 0)
    inside = ((row > 0) | (strip > 0)) & ((row != rows + 1) | (strip < strips - 1))
    scale = jnp.where(inside, 1.0 / 64.0, 0.0)
    scale_front = jnp.where(inside & (depth > 0), 1.0 / 64.0, 0.0)
    scale_back = jnp.where(inside & (depth < groups - 1), 1.0 / 64.0, 0.0)
    for scalar in scalars:
        scalar.wait()
    light = [light_ref[0] / 32.0, light_ref[1] / 32.0, light_ref[2] / 32.0]

    def smooth_slices(t, low, high):
        def over_rows(z):
            return (
                ext_field[t, z, EDGE - 2:EDGE - 2 + tall]
                + ext_field[t, z, EDGE:EDGE + tall]
                + 2.0 * ext_field[t, z, EDGE - 1:EDGE - 1 + tall]
            )

        one, two = over_rows(low), over_rows(low + 1)
        for z in range(low, high):
            three = over_rows(z + 2)
            weight = scale_front if z == 0 else scale_back if z == slabs + 1 else scale
            smooth[t, z] = jnp.where(weight > 0.0, (one + three + 2.0 * two) * weight, 0.0)
            one, two = two, three

    def gradients(t, low, high):
        def rows_of(z):
            under = smooth[t, z, 0:rows]
            middle = smooth[t, z, 1:rows + 1]
            over = smooth[t, z, 2:rows + 2]
            return under + over + 2.0 * middle, over - under

        one, two = rows_of(low), rows_of(low + 1)
        for z in range(low, high):
            three = rows_of(z + 2)
            across = (
                light[0] * (one[1] + three[1] + 2.0 * two[1])
                + light[1] * (three[0] - one[0])
            )
            along = light[2] * (one[0] + three[0] + 2.0 * two[0])
            ahead[t, z] = across + along
            behind[t + 1, z] = across - along
            one, two = two, three

    to_double = 2.0 / math.log(2.0)
    thinning = ext_ref[0] * (-1.0 / math.log(2.0))
    slope = [0.5 * color_ref[0, k] for k in range(3)]
    offset = [0.5 * color_ref[1, k] for k in range(3)]

    def render(t, low, high):
        density = jnp.zeros((rows, LANES), jnp.float32)
        passed = jnp.ones((rows, LANES), jnp.float32)
        total = jnp.zeros((rows, LANES), jnp.float32)
        tinted = [jnp.zeros((rows, LANES), jnp.float32) for _ in range(3)]
        for z in range(low, high):
            up, down = ahead[t, z], behind[t + 1, z]
            facing = (
                next_lane(up, ahead[t + 1, z], lane)
                + previous_lane(down, behind[t, z], lane)
                + (up + down)
            )
            stretch = 1.0 + facing * facing
            guess = pl.reciprocal(stretch, approx=True)
            inverse = guess * (2.0 - stretch * guess)
            field = smooth[t, z + 1, 1:rows + 1]
            density += jnp.log(1.0 + jnp.exp2(to_double * field))
            beyond = jnp.exp2(thinning * density)
            weight = (passed - beyond) * (1.0 - 0.7 * inverse)
            passed = beyond
            total += weight
            for k in range(3):
                tinted[k] += weight * jnp.tanh(slope[k] * field + offset[k])
        return [0.5 * (total + tinted[k]) for k in range(3)] + [passed]

    def over(front, back):
        return [front[k] + front[3] * back[k] for k in range(3)] + [front[3] * back[3]]

    inner = (2, max(2, slabs - 2))

    def inner_field(t, carry):
        smooth_slices(t, inner[0], inner[1] + 2)
        gradients(t, *inner)
        return carry

    def inner_render(t, carry):
        value = render(t, *inner)
        for k in range(4):
            picture[t, k] = value[k]
        return carry

    def outer_field(t, carry):
        smooth_slices(t, 0, inner[0])
        smooth_slices(t, inner[1] + 2, slabs + 2)
        gradients(t, 0, inner[0])
        gradients(t, inner[1], slabs)
        return carry

    def outer_render(t, carry):
        value = over(render(t, 0, inner[0]), [picture[t, k] for k in range(4)])
        value = over(value, render(t, inner[1], slabs))
        for k in range(4):
            picture[t, k] = value[k]
        return carry

    def swap(level, other, part, sender):
        radix, stride = levels[level][:2]
        digit = depth // stride % radix
        source, slot = (other, digit) if sender else (digit, other)
        return pltpu.make_async_remote_copy(
            src_ref=sent[level].at[source, part],
            dst_ref=got[level].at[slot, part],
            send_sem=swap_send.at[level, source, part],
            recv_sem=swap_recv.at[level, slot, part],
            device_id=(depth + (other - digit) * stride, strip),
            device_id_type=MESH,
        )

    def dispatch(level, j, part):
        radix, stride = levels[level][:2]
        digit = depth // stride % radix

        @pl.when(digit != j)
        def _():
            swap(level, j, part, True).start()

        @pl.when(digit == j)
        def _():
            got[level][j, part] = sent[level][j, part]

    def blocks_of(level, j, part):
        radix, _, _, width, _ = levels[level]
        each = width // block
        return [q * radix + j for q in range(part * each, (part + 1) * each)]

    def fill(level, j, part, tile_of, span):
        width = levels[level][3]
        per, count = packing(width)
        for c in range(count):
            sent[level][j, part, c] = place(
                [
                    (
                        tile_of(k, b * block // span), b * block % span,
                        (k - c * per) * width + i * block, block,
                    )
                    for k in range(c * per, min(4, (c + 1) * per))
                    for i, b in enumerate(blocks_of(level, j, part))
                ],
                lane,
            )

    wait_halos(0, over_strip)
    lax.fori_loop(0, tiles, inner_field, 0)
    lax.fori_loop(0, tiles, inner_render, 0)

    for c in range(stages):
        leave_halos(c, over_depth)
        if c + 2 < len(spans):
            start_halos(c + 2, over_depth)
        if c == 0:
            wait_halos(0, over_depth)
        wait_halos(c + 1, over_depth)
        lax.fori_loop(starts[c], ends[c], outer_field, 0)
        lax.fori_loop(c * per_stage, (c + 1) * per_stage, outer_render, 0)
        for j in range(first[0]):
            fill(0, j, c, lambda k, t: picture[t, k], LANES)
            dispatch(0, j, c)

    current = []
    for level, (radix, stride, _, width, parts) in enumerate(levels):
        per, _ = packing(width)
        digit = depth // stride % radix
        current, gone = [], set()
        for part in range(parts):
            for step in range(1, radix):
                swap(level, (digit + step) % radix, part, False).wait_recv()

            def channel(j, k):
                tile = got[level][j, part, k // per]
                shift = -(k % per) * width % LANES
                return pltpu.roll(tile, shift, 1) if shift else tile

            value = [channel(0, k) for k in range(4)]
            for j in range(1, radix):
                value = over(value, [channel(j, k) for k in range(4)])
            current.append(value)
            if level + 1 < len(levels):
                for j in range(levels[level + 1][0]):
                    for later in range(levels[level + 1][4]):
                        needed = [b * block // width for b in blocks_of(level + 1, j, later)]
                        if (j, later) not in gone and max(needed) <= part:
                            gone.add((j, later))
                            fill(level + 1, j, later, lambda k, t: current[t][k], width)
                            dispatch(level + 1, j, later)

    for k in range(4):
        out_ref[k] = current[0][k][:, :block]

    leave_halos(0, over_strip)
    leave_halos(stages, over_depth)
    for level, (radix, stride, _, _, parts) in enumerate(levels):
        digit = depth // stride % radix
        for part in range(parts):
            for step in range(1, radix):
                swap(level, (digit + step) % radix, part, True).wait_send()


def local(volume, extinction, color_map, light_direction):
    rows, slabs, columns = volume.shape
    groups, strips = lax.axis_size("depth"), lax.axis_size("strip")
    tiles, block = columns // LANES, columns // groups
    levels = plan(groups, columns)
    stages = levels[0][4]
    f32 = jnp.float32
    buffers = []
    for radix, _, _, width, parts in levels:
        buffers.append(pltpu.VMEM((radix, parts, packing(width)[1], rows, LANES), f32))
    most = max(level[4] for level in levels)
    image = pl.pallas_call(
        functools.partial(kernel, groups, strips, rows, slabs, columns),
        out_shape=jax.ShapeDtypeStruct((4, rows, block), f32),
        in_specs=[pl.BlockSpec(memory_space=pl.ANY)] * 4,
        out_specs=pl.BlockSpec(memory_space=pltpu.VMEM),
        scratch_shapes=[
            pltpu.SMEM((1,), f32),
            pltpu.SMEM((2, 3), f32),
            pltpu.SMEM((3,), f32),
            pltpu.VMEM((tiles, rows * slabs, LANES), f32),
            pltpu.VMEM((tiles, slabs + 4, rows + 2 * EDGE, LANES), f32),
            pltpu.VMEM((tiles, slabs + 2, rows + 8, LANES), f32),
            pltpu.VMEM((tiles + 1, slabs, rows, LANES), f32),
            pltpu.VMEM((tiles + 1, slabs, rows, LANES), f32),
            pltpu.VMEM((tiles, 4, rows, LANES), f32),
            *buffers,
            *buffers,
            pltpu.SemaphoreType.DMA((tiles,)),
            pltpu.SemaphoreType.DMA((3,)),
            pltpu.SemaphoreType.DMA((stages + 1, len(SIDES))),
            pltpu.SemaphoreType.DMA((stages + 1, len(SIDES))),
            pltpu.SemaphoreType.DMA((len(levels), 4, most)),
            pltpu.SemaphoreType.DMA((len(levels), 4, most)),
        ],
        compiler_params=pltpu.CompilerParams(
            collective_id=0, has_side_effects=True, vmem_limit_bytes=56 * 1024 * 1024
        ),
    )(extinction, color_map.T, light_direction, volume.reshape(rows * slabs, columns))
    last = lax.broadcasted_iota(jnp.int32, image.shape, 0) == 3
    return jnp.where(last, 1.0 - image, image)


def solution(mesh):
    in_specs = (P("strip", "depth", None), P(), P(), P())
    out_specs = P(None, "strip", "depth")
    return jax.shard_map(local, mesh=mesh, in_specs=in_specs, out_specs=out_specs, check_vma=False)
```

```python
import functools
import math

import jax
import jax.numpy as jnp
from jax import lax
from jax.experimental import pallas as pl
from jax.experimental.pallas import tpu as pltpu
from jax.sharding import PartitionSpec as P

LANES = 128
EDGE = 8
MESH = pl.DeviceIdType.MESH
SIDES = [(dz, ds) for dz in (-1, 0, 1) for ds in (-1, 0, 1) if (dz, ds) != (0, 0)]


def radices_of(count):
    found = []
    while count > 1:
        radix = 4 if count % 4 == 0 else 2
        found.append(radix)
        count //= radix
    return found


def next_lane(here, after, lane):
    return pltpu.roll(jnp.where(lane == 0, after, here), LANES - 1, here.ndim - 1)


def previous_lane(here, before, lane):
    return pltpu.roll(jnp.where(lane == LANES - 1, before, here), 1, here.ndim - 1)


def place(parts, lane):
    result = None
    for tile, source, target, width in parts:
        shift = (target - source) % LANES
        moved = pltpu.roll(tile, shift, 1) if shift else tile
        if result is None:
            result = moved
        else:
            result = jnp.where((lane >= target) & (lane < target + width), moved, result)
    return result


def stages_of(groups, columns):
    return max(1, min(columns // LANES // 4, columns // (radices_of(groups)[0] * columns // groups)))


def plan(groups, columns):
    levels, stride, held = [], 1, columns
    for radix in radices_of(groups):
        width = held // radix
        part = min(width, LANES)
        if not levels:
            part = min(part, width // stages_of(groups, columns))
        levels.append((radix, stride, width, part, width // part))
        stride *= radix
        held = width
    return levels


def packing(part):
    per = min(4, LANES // part)
    return per, -(-4 // per)


def kernel(groups, strips, rows, slabs, columns,
           ext_hbm, color_hbm, light_hbm, vol_ref, out_ref,
           ext_ref, color_ref, light_ref, vol, ext_field, smooth, ahead, behind, picture, *rest):
    levels = plan(groups, columns)
    sent = rest[:len(levels)]
    got = rest[len(levels):2 * len(levels)]
    load_sem, small_sem, halo_send, halo_recv, swap_send, swap_recv = rest[2 * len(levels):]
    tiles = columns // LANES
    block = columns // groups
    depth, strip = lax.axis_index("depth"), lax.axis_index("strip")
    lane = lax.broadcasted_iota(jnp.int32, (rows, LANES), 1)
    lane8 = lax.broadcasted_iota(jnp.int32, (8, LANES), 1)
    tall = rows + 8

    loads = [
        pltpu.make_async_copy(vol_ref.at[:, pl.ds(t * LANES, LANES)], vol.at[t], load_sem.at[t])
        for t in range(tiles)
    ]
    for load in loads:
        load.start()
    scalars = [
        pltpu.make_async_copy(source, target, small_sem.at[i])
        for i, (source, target) in enumerate(
            [(ext_hbm, ext_ref), (color_hbm, color_ref), (light_hbm, light_ref)])
    ]
    for scalar in scalars:
        scalar.start()

    def there(dz, ds):
        return (depth + dz >= 0) & (depth + dz < groups) & (strip + ds >= 0) & (strip + ds < strips)

    barrier = pltpu.get_barrier_semaphore()
    expected = 0
    for dz, ds in SIDES:
        expected = expected + jnp.where(there(dz, ds), 1, 0)

        @pl.when(there(dz, ds))
        def _(dz=dz, ds=ds):
            pl.semaphore_signal(barrier, inc=1, device_id=(depth + dz, strip + ds), device_id_type=MESH)

    for radix, stride, _, _, _ in levels:
        digit = depth // stride % radix
        for step in range(1, radix):
            other = depth + ((digit + step) % radix - digit) * stride
            pl.semaphore_signal(barrier, inc=1, device_id=(other, strip), device_id_type=MESH)
            expected = expected + 1

    @pl.when(depth == 0)
    def _():
        ext_field[:, 0:2] = jnp.zeros((tiles, 2, rows + 2 * EDGE, LANES), jnp.float32)

    @pl.when(depth == groups - 1)
    def _():
        ext_field[:, slabs + 2:] = jnp.zeros((tiles, 2, rows + 2 * EDGE, LANES), jnp.float32)

    @pl.when(strip == 0)
    def _():
        ext_field[:, :, 0:EDGE] = jnp.zeros((tiles, slabs + 4, EDGE, LANES), jnp.float32)

    @pl.when(strip == strips - 1)
    def _():
        ext_field[:, :, rows + EDGE:] = jnp.zeros((tiles, slabs + 4, EDGE, LANES), jnp.float32)

    ahead[tiles] = jnp.zeros((slabs, rows, LANES), jnp.float32)
    behind[0] = jnp.zeros((slabs, rows, LANES), jnp.float32)

    for load in loads:
        load.wait()

    first = levels[0]
    stages = first[4]
    per_stage = tiles // stages
    ends = [min(tiles, (c + 1) * per_stage + 1) for c in range(stages)]
    starts = [0] + ends[:-1]

    def halo(c, index, sender):
        dz, ds = SIDES[index]
        low, high = (starts[c], ends[c]) if ds == 0 else (0, tiles)
        span = pl.ds(low, high - low)
        z_from, z_to, z_count = {
            -1: (2, slabs + 2, 2), 0: (2, 2, slabs), 1: (slabs, 0, 2)}[dz]
        r_from, r_to, r_count = {
            -1: (EDGE, EDGE + rows, 2), 0: (EDGE, EDGE, rows), 1: (EDGE + rows - 2, EDGE - 2, 2)}[ds]
        sign = 1 if sender else -1
        return pltpu.make_async_remote_copy(
            src_ref=ext_field.at[span, pl.ds(z_from, z_count), pl.ds(r_from, r_count)],
            dst_ref=ext_field.at[span, pl.ds(z_to, z_count), pl.ds(r_to, r_count)],
            send_sem=halo_send.at[c, index],
            recv_sem=halo_recv.at[c, index],
            device_id=(depth + sign * dz, strip + sign * ds),
            device_id_type=MESH,
        )

    def blur_columns(z, carry):
        for h in range(rows // 8):
            cells = [vol[t, pl.ds(8 * h * slabs + z, 8, stride=slabs), :] for t in range(tiles)]
            nothing = jnp.zeros_like(cells[0])
            for t in range(tiles):
                before = cells[t - 1] if t > 0 else nothing
                after = cells[t + 1] if t < tiles - 1 else nothing
                ext_field[t, z + 2, EDGE + 8 * h:EDGE + 8 * h + 8] = (
                    next_lane(cells[t], after, lane8)
                    + previous_lane(cells[t], before, lane8)
                    + 2.0 * cells[t]
                )
        return carry

    def start_halos(c, chosen):
        for index in chosen:
            dz, ds = SIDES[index]

            @pl.when(there(dz, ds))
            def _(c=c, index=index):
                halo(c, index, True).start()

    def leave_halos(c, chosen):
        for index in chosen:
            dz, ds = SIDES[index]

            @pl.when(there(dz, ds))
            def _(c=c, index=index):
                halo(c, index, True).wait_send()

    def wait_halos(c, chosen):
        for index in chosen:
            dz, ds = SIDES[index]

            @pl.when(there(-dz, -ds))
            def _(c=c, index=index):
                halo(c, index, False).wait_recv()

    straight = [i for i, (_, ds) in enumerate(SIDES) if ds == 0]
    corners = [i for i, (dz, ds) in enumerate(SIDES) if dz != 0 and ds != 0]
    over_strip = [i for i, (dz, _) in enumerate(SIDES) if dz == 0]
    lax.fori_loop(0, 2, blur_columns, 0)
    lax.fori_loop(slabs - 2, slabs, blur_columns, 0)
    pl.semaphore_wait(barrier, expected)
    start_halos(0, straight + corners)
    lax.fori_loop(2, slabs - 2, blur_columns, 0)
    start_halos(0, over_strip)

    row = lax.broadcasted_iota(jnp.int32, (tall, LANES), 0)
    inside = ((row > 0) | (strip > 0)) & ((row != rows + 1) | (strip < strips - 1))
    scale = jnp.where(inside, 1.0 / 64.0, 0.0)
    scale_front = jnp.where(inside & (depth > 0), 1.0 / 64.0, 0.0)
    scale_back = jnp.where(inside & (depth < groups - 1), 1.0 / 64.0, 0.0)
    for scalar in scalars:
        scalar.wait()
    light = [light_ref[0] / 32.0, light_ref[1] / 32.0, light_ref[2] / 32.0]

    def smooth_slices(t, low, high):
        def over_rows(z):
            return (
                ext_field[t, z, EDGE - 2:EDGE - 2 + tall]
                + ext_field[t, z, EDGE:EDGE + tall]
                + 2.0 * ext_field[t, z, EDGE - 1:EDGE - 1 + tall]
            )

        one, two = over_rows(low), over_rows(low + 1)
        for z in range(low, high):
            three = over_rows(z + 2)
            weight = scale_front if z == 0 else scale_back if z == slabs + 1 else scale
            smooth[t, z] = jnp.where(weight > 0.0, (one + three + 2.0 * two) * weight, 0.0)
            one, two = two, three

    def gradients(t, low, high):
        def rows_of(z):
            under = smooth[t, z, 0:rows]
            middle = smooth[t, z, 1:rows + 1]
            over = smooth[t, z, 2:rows + 2]
            return under + over + 2.0 * middle, over - under

        one, two = rows_of(low), rows_of(low + 1)
        for z in range(low, high):
            three = rows_of(z + 2)
            across = (
                light[0] * (one[1] + three[1] + 2.0 * two[1])
                + light[1] * (three[0] - one[0])
            )
            along = light[2] * (one[0] + three[0] + 2.0 * two[0])
            ahead[t, z] = across + along
            behind[t + 1, z] = across - along
            one, two = two, three

    to_double = 2.0 / math.log(2.0)
    thinning = ext_ref[0] * (-1.0 / math.log(2.0))
    slope = [0.5 * color_ref[0, k] for k in range(3)]
    offset = [0.5 * color_ref[1, k] for k in range(3)]

    def render(t, low, high):
        density = jnp.zeros((rows, LANES), jnp.float32)
        passed = jnp.ones((rows, LANES), jnp.float32)
        total = jnp.zeros((rows, LANES), jnp.float32)
        tinted = [jnp.zeros((rows, LANES), jnp.float32) for _ in range(3)]
        for z in range(low, high):
            up, down = ahead[t, z], behind[t + 1, z]
            facing = (
                next_lane(up, ahead[t + 1, z], lane)
                + previous_lane(down, behind[t, z], lane)
                + (up + down)
            )
            stretch = 1.0 + facing * facing
            guess = pl.reciprocal(stretch, approx=True)
            inverse = guess * (2.0 - stretch * guess)
            field = smooth[t, z + 1, 1:rows + 1]
            density += jnp.log(1.0 + jnp.exp2(to_double * field))
            beyond = jnp.exp2(thinning * density)
            weight = (passed - beyond) * (1.0 - 0.7 * inverse)
            passed = beyond
            total += weight
            for k in range(3):
                tinted[k] += weight * jnp.tanh(slope[k] * field + offset[k])
        return [0.5 * (total + tinted[k]) for k in range(3)] + [passed]

    def over(front, back):
        return [front[k] + front[3] * back[k] for k in range(3)] + [front[3] * back[3]]

    inner = (2, max(2, slabs - 2))

    def inner_field(t, carry):
        smooth_slices(t, inner[0], inner[1] + 2)
        gradients(t, *inner)
        return carry

    def inner_render(t, carry):
        value = render(t, *inner)
        for k in range(4):
            picture[t, k] = value[k]
        return carry

    def outer_field(t, carry):
        smooth_slices(t, 0, inner[0])
        smooth_slices(t, inner[1] + 2, slabs + 2)
        gradients(t, 0, inner[0])
        gradients(t, inner[1], slabs)
        return carry

    def outer_render(t, carry):
        value = over(render(t, 0, inner[0]), [picture[t, k] for k in range(4)])
        value = over(value, render(t, inner[1], slabs))
        for k in range(4):
            picture[t, k] = value[k]
        return carry

    def swap(level, other, part, sender):
        radix, stride = levels[level][:2]
        digit = depth // stride % radix
        source, slot = (other, digit) if sender else (digit, other)
        return pltpu.make_async_remote_copy(
            src_ref=sent[level].at[source, part],
            dst_ref=got[level].at[slot, part],
            send_sem=swap_send.at[level, source, part],
            recv_sem=swap_recv.at[level, slot, part],
            device_id=(depth + (other - digit) * stride, strip),
            device_id_type=MESH,
        )

    def dispatch(level, j, part):
        radix, stride = levels[level][:2]
        digit = depth // stride % radix

        @pl.when(digit != j)
        def _():
            swap(level, j, part, True).start()

        @pl.when(digit == j)
        def _():
            got[level][j, part] = sent[level][j, part]

    def blocks_of(level, j, part):
        radix, _, _, width, _ = levels[level]
        each = width // block
        return [q * radix + j for q in range(part * each, (part + 1) * each)]

    def fill(level, j, part, tile_of, span):
        width = levels[level][3]
        per, count = packing(width)
        for c in range(count):
            sent[level][j, part, c] = place(
                [
                    (
                        tile_of(k, b * block // span), b * block % span,
                        (k - c * per) * width + i * block, block,
                    )
                    for k in range(c * per, min(4, (c + 1) * per))
                    for i, b in enumerate(blocks_of(level, j, part))
                ],
                lane,
            )

    wait_halos(0, over_strip)
    lax.fori_loop(0, tiles, inner_field, 0)
    lax.fori_loop(0, tiles, inner_render, 0)

    for c in range(stages):
        leave_halos(c, straight)
        if c + 1 < stages:
            start_halos(c + 1, straight)
        wait_halos(c, straight + corners if c == 0 else straight)
        lax.fori_loop(starts[c], ends[c], outer_field, 0)
        lax.fori_loop(c * per_stage, (c + 1) * per_stage, outer_render, 0)
        for j in range(first[0]):
            fill(0, j, c, lambda k, t: picture[t, k], LANES)
            dispatch(0, j, c)

    current = []
    for level, (radix, stride, _, width, parts) in enumerate(levels):
        per, _ = packing(width)
        digit = depth // stride % radix
        current, gone = [], set()
        for part in range(parts):
            for step in range(1, radix):
                swap(level, (digit + step) % radix, part, False).wait_recv()

            def channel(j, k):
                tile = got[level][j, part, k // per]
                shift = -(k % per) * width % LANES
                return pltpu.roll(tile, shift, 1) if shift else tile

            value = [channel(0, k) for k in range(4)]
            for j in range(1, radix):
                value = over(value, [channel(j, k) for k in range(4)])
            current.append(value)
            if level + 1 < len(levels):
                for j in range(levels[level + 1][0]):
                    for later in range(levels[level + 1][4]):
                        needed = [b * block // width for b in blocks_of(level + 1, j, later)]
                        if (j, later) not in gone and max(needed) <= part:
                            gone.add((j, later))
                            fill(level + 1, j, later, lambda k, t: current[t][k], width)
                            dispatch(level + 1, j, later)

    for k in range(4):
        out_ref[k] = current[0][k][:, :block]

    leave_halos(0, over_strip + corners)
    for level, (radix, stride, _, _, parts) in enumerate(levels):
        digit = depth // stride % radix
        for part in range(parts):
            for step in range(1, radix):
                swap(level, (digit + step) % radix, part, True).wait_send()


def local(volume, extinction, color_map, light_direction):
    rows, slabs, columns = volume.shape
    groups, strips = lax.axis_size("depth"), lax.axis_size("strip")
    tiles, block = columns // LANES, columns // groups
    levels = plan(groups, columns)
    stages = levels[0][4]
    f32 = jnp.float32
    buffers = []
    for radix, _, _, width, parts in levels:
        buffers.append(pltpu.VMEM((radix, parts, packing(width)[1], rows, LANES), f32))
    most = max(level[4] for level in levels)
    image = pl.pallas_call(
        functools.partial(kernel, groups, strips, rows, slabs, columns),
        out_shape=jax.ShapeDtypeStruct((4, rows, block), f32),
        in_specs=[pl.BlockSpec(memory_space=pl.ANY)] * 4,
        out_specs=pl.BlockSpec(memory_space=pltpu.VMEM),
        scratch_shapes=[
            pltpu.SMEM((1,), f32),
            pltpu.SMEM((2, 3), f32),
            pltpu.SMEM((3,), f32),
            pltpu.VMEM((tiles, rows * slabs, LANES), f32),
            pltpu.VMEM((tiles, slabs + 4, rows + 2 * EDGE, LANES), f32),
            pltpu.VMEM((tiles, slabs + 2, rows + 8, LANES), f32),
            pltpu.VMEM((tiles + 1, slabs, rows, LANES), f32),
            pltpu.VMEM((tiles + 1, slabs, rows, LANES), f32),
            pltpu.VMEM((tiles, 4, rows, LANES), f32),
            *buffers,
            *buffers,
            pltpu.SemaphoreType.DMA((tiles,)),
            pltpu.SemaphoreType.DMA((3,)),
            pltpu.SemaphoreType.DMA((stages, len(SIDES))),
            pltpu.SemaphoreType.DMA((stages, len(SIDES))),
            pltpu.SemaphoreType.DMA((len(levels), 4, most)),
            pltpu.SemaphoreType.DMA((len(levels), 4, most)),
        ],
        compiler_params=pltpu.CompilerParams(
            collective_id=0, has_side_effects=True, vmem_limit_bytes=56 * 1024 * 1024
        ),
    )(extinction, color_map.T, light_direction, volume.reshape(rows * slabs, columns))
    last = lax.broadcasted_iota(jnp.int32, image.shape, 0) == 3
    return jnp.where(last, 1.0 - image, image)


def solution(mesh):
    in_specs = (P("strip", "depth", None), P(), P(), P())
    out_specs = P(None, "strip", "depth")
    return jax.shard_map(local, mesh=mesh, in_specs=in_specs, out_specs=out_specs, check_vma=False)
```

```python
import functools
import math

import jax
import jax.numpy as jnp
from jax import lax
from jax.experimental import pallas as pl
from jax.experimental.pallas import tpu as pltpu
from jax.sharding import PartitionSpec as P

LANES = 128
EDGE = 8
MESH = pl.DeviceIdType.MESH
SIDES = [(dz, ds) for dz in (-1, 0, 1) for ds in (-1, 0, 1) if (dz, ds) != (0, 0)]


def radices_of(count):
    found = []
    while count > 1:
        radix = 4 if count % 4 == 0 else 2
        found.append(radix)
        count //= radix
    return found


def next_lane(here, after, lane):
    return pltpu.roll(jnp.where(lane == 0, after, here), LANES - 1, here.ndim - 1)


def previous_lane(here, before, lane):
    return pltpu.roll(jnp.where(lane == LANES - 1, before, here), 1, here.ndim - 1)


def place(parts, lane):
    result = None
    for tile, source, target, width in parts:
        shift = (target - source) % LANES
        moved = pltpu.roll(tile, shift, 1) if shift else tile
        if result is None:
            result = moved
        else:
            result = jnp.where((lane >= target) & (lane < target + width), moved, result)
    return result


def plan(groups, columns):
    levels, stride, held = [], 1, columns
    for radix in radices_of(groups):
        levels.append((radix, stride, held, held // radix))
        stride *= radix
        held //= radix
    return levels


def piece_tiles(width):
    if width >= LANES:
        return 1, 4 * (width // LANES)
    per = min(4, LANES // width)
    return per, -(-4 // per)


def kernel(groups, strips, rows, slabs, columns,
           ext_hbm, color_hbm, light_hbm, vol_ref, out_ref,
           ext_ref, color_ref, light_ref, vol, ext_field, smooth, ahead, behind, picture, *rest):
    levels = plan(groups, columns)
    sent = rest[:len(levels)]
    got = rest[len(levels):2 * len(levels)]
    load_sem, small_sem, halo_send, halo_recv, swap_send, swap_recv = rest[2 * len(levels):]
    tiles = columns // LANES
    block = columns // groups
    depth, strip = lax.axis_index("depth"), lax.axis_index("strip")
    lane = lax.broadcasted_iota(jnp.int32, (rows, LANES), 1)
    lane8 = lax.broadcasted_iota(jnp.int32, (8, LANES), 1)
    tall = rows + 8

    loads = [
        pltpu.make_async_copy(vol_ref.at[:, pl.ds(t * LANES, LANES)], vol.at[t], load_sem.at[t])
        for t in range(tiles)
    ]
    for load in loads:
        load.start()
    scalars = [
        pltpu.make_async_copy(source, target, small_sem.at[i])
        for i, (source, target) in enumerate(
            [(ext_hbm, ext_ref), (color_hbm, color_ref), (light_hbm, light_ref)])
    ]
    for scalar in scalars:
        scalar.start()

    def there(dz, ds):
        return (depth + dz >= 0) & (depth + dz < groups) & (strip + ds >= 0) & (strip + ds < strips)

    def partner(level, step):
        radix, stride, _, _ = levels[level]
        digit = depth // stride % radix
        other = (digit + step) % radix
        return digit, other, depth + (other - digit) * stride

    barrier = pltpu.get_barrier_semaphore()
    expected = 0
    for dz, ds in SIDES:
        expected = expected + jnp.where(there(dz, ds), 1, 0)

        @pl.when(there(dz, ds))
        def _(dz=dz, ds=ds):
            pl.semaphore_signal(barrier, inc=1, device_id=(depth + dz, strip + ds), device_id_type=MESH)

    for level, (radix, _, _, _) in enumerate(levels):
        for step in range(1, radix):
            pl.semaphore_signal(
                barrier, inc=1, device_id=(partner(level, step)[2], strip), device_id_type=MESH
            )
            expected = expected + 1

    @pl.when(depth == 0)
    def _():
        ext_field[:, 0:2] = jnp.zeros((tiles, 2, rows + 2 * EDGE, LANES), jnp.float32)

    @pl.when(depth == groups - 1)
    def _():
        ext_field[:, slabs + 2:] = jnp.zeros((tiles, 2, rows + 2 * EDGE, LANES), jnp.float32)

    @pl.when(strip == 0)
    def _():
        ext_field[:, :, 0:EDGE] = jnp.zeros((tiles, slabs + 4, EDGE, LANES), jnp.float32)

    @pl.when(strip == strips - 1)
    def _():
        ext_field[:, :, rows + EDGE:] = jnp.zeros((tiles, slabs + 4, EDGE, LANES), jnp.float32)

    ahead[tiles] = jnp.zeros((slabs, rows, LANES), jnp.float32)
    behind[0] = jnp.zeros((slabs, rows, LANES), jnp.float32)

    for load in loads:
        load.wait()

    first = levels[0]
    stages = max(1, first[3] // LANES)
    per_stage = tiles // stages
    ends = [min(tiles, (c + 1) * per_stage + 1) for c in range(stages)]
    starts = [0] + ends[:-1]

    def halo(c, index, sender):
        dz, ds = SIDES[index]
        span = pl.ds(starts[c], ends[c] - starts[c])
        z_from, z_to, z_count = {
            -1: (2, slabs + 2, 2), 0: (2, 2, slabs), 1: (slabs, 0, 2)}[dz]
        r_from, r_to, r_count = {
            -1: (EDGE, EDGE + rows, 2), 0: (EDGE, EDGE, rows), 1: (EDGE + rows - 2, EDGE - 2, 2)}[ds]
        sign = 1 if sender else -1
        return pltpu.make_async_remote_copy(
            src_ref=ext_field.at[span, pl.ds(z_from, z_count), pl.ds(r_from, r_count)],
            dst_ref=ext_field.at[span, pl.ds(z_to, z_count), pl.ds(r_to, r_count)],
            send_sem=halo_send.at[c, index],
            recv_sem=halo_recv.at[c, index],
            device_id=(depth + sign * dz, strip + sign * ds),
            device_id_type=MESH,
        )

    def blur_columns(z, carry):
        for h in range(rows // 8):
            cells = [vol[t, pl.ds(8 * h * slabs + z, 8, stride=slabs), :] for t in range(tiles)]
            nothing = jnp.zeros_like(cells[0])
            for t in range(tiles):
                before = cells[t - 1] if t > 0 else nothing
                after = cells[t + 1] if t < tiles - 1 else nothing
                ext_field[t, z + 2, EDGE + 8 * h:EDGE + 8 * h + 8] = (
                    next_lane(cells[t], after, lane8)
                    + previous_lane(cells[t], before, lane8)
                    + 2.0 * cells[t]
                )
        return carry

    def start_halos(c, chosen):
        for index in chosen:
            dz, ds = SIDES[index]

            @pl.when(there(dz, ds))
            def _(c=c, index=index):
                halo(c, index, True).start()

    def leave_halos(c, chosen):
        for index in chosen:
            dz, ds = SIDES[index]

            @pl.when(there(dz, ds))
            def _(c=c, index=index):
                halo(c, index, True).wait_send()

    def wait_halos(c, chosen):
        for index in chosen:
            dz, ds = SIDES[index]

            @pl.when(there(-dz, -ds))
            def _(c=c, index=index):
                halo(c, index, False).wait_recv()

    over_depth = [i for i, (dz, _) in enumerate(SIDES) if dz != 0]
    over_strip = [i for i, (dz, _) in enumerate(SIDES) if dz == 0]
    lax.fori_loop(0, 2, blur_columns, 0)
    lax.fori_loop(slabs - 2, slabs, blur_columns, 0)
    pl.semaphore_wait(barrier, expected)
    start_halos(0, over_depth)
    lax.fori_loop(2, slabs - 2, blur_columns, 0)
    for c in range(stages):
        start_halos(c, over_strip)

    row = lax.broadcasted_iota(jnp.int32, (tall, LANES), 0)
    inside = ((row > 0) | (strip > 0)) & ((row != rows + 1) | (strip < strips - 1))
    scale = jnp.where(inside, 1.0 / 64.0, 0.0)
    scale_front = jnp.where(inside & (depth > 0), 1.0 / 64.0, 0.0)
    scale_back = jnp.where(inside & (depth < groups - 1), 1.0 / 64.0, 0.0)
    for scalar in scalars:
        scalar.wait()
    light = [light_ref[0] / 32.0, light_ref[1] / 32.0, light_ref[2] / 32.0]

    def smooth_slices(t, low, high):
        def over_rows(z):
            return (
                ext_field[t, z, EDGE - 2:EDGE - 2 + tall]
                + ext_field[t, z, EDGE:EDGE + tall]
                + 2.0 * ext_field[t, z, EDGE - 1:EDGE - 1 + tall]
            )

        one, two = over_rows(low), over_rows(low + 1)
        for z in range(low, high):
            three = over_rows(z + 2)
            weight = scale_front if z == 0 else scale_back if z == slabs + 1 else scale
            smooth[t, z] = jnp.where(weight > 0.0, (one + three + 2.0 * two) * weight, 0.0)
            one, two = two, three

    def gradients(t, low, high):
        def rows_of(z):
            under = smooth[t, z, 0:rows]
            middle = smooth[t, z, 1:rows + 1]
            over = smooth[t, z, 2:rows + 2]
            return under + over + 2.0 * middle, over - under

        one, two = rows_of(low), rows_of(low + 1)
        for z in range(low, high):
            three = rows_of(z + 2)
            across = (
                light[0] * (one[1] + three[1] + 2.0 * two[1])
                + light[1] * (three[0] - one[0])
            )
            along = light[2] * (one[0] + three[0] + 2.0 * two[0])
            ahead[t, z] = across + along
            behind[t + 1, z] = across - along
            one, two = two, three

    to_double = 2.0 / math.log(2.0)
    thinning = ext_ref[0] * (-1.0 / math.log(2.0))
    slope = [0.5 * color_ref[0, k] for k in range(3)]
    offset = [0.5 * color_ref[1, k] for k in range(3)]

    def render(t, low, high):
        density = jnp.zeros((rows, LANES), jnp.float32)
        passed = jnp.ones((rows, LANES), jnp.float32)
        total = jnp.zeros((rows, LANES), jnp.float32)
        tinted = [jnp.zeros((rows, LANES), jnp.float32) for _ in range(3)]
        for z in range(low, high):
            up, down = ahead[t, z], behind[t + 1, z]
            facing = (
                next_lane(up, ahead[t + 1, z], lane)
                + previous_lane(down, behind[t, z], lane)
                + (up + down)
            )
            stretch = 1.0 + facing * facing
            guess = pl.reciprocal(stretch, approx=True)
            inverse = guess * (2.0 - stretch * guess)
            field = smooth[t, z + 1, 1:rows + 1]
            density += jnp.log(1.0 + jnp.exp2(to_double * field))
            beyond = jnp.exp2(thinning * density)
            weight = (passed - beyond) * (1.0 - 0.7 * inverse)
            passed = beyond
            total += weight
            for k in range(3):
                tinted[k] += weight * jnp.tanh(slope[k] * field + offset[k])
        return [0.5 * (total + tinted[k]) for k in range(3)] + [passed]

    def over(front, back):
        return [front[k] + front[3] * back[k] for k in range(3)] + [front[3] * back[3]]

    inner = (2, max(2, slabs - 2))

    def inner_field(t, carry):
        smooth_slices(t, inner[0], inner[1] + 2)
        gradients(t, *inner)
        return carry

    def inner_render(t, carry):
        value = render(t, *inner)
        for k in range(4):
            picture[t, k] = value[k]
        return carry

    def outer_field(t, carry):
        smooth_slices(t, 0, inner[0])
        smooth_slices(t, inner[1] + 2, slabs + 2)
        gradients(t, 0, inner[0])
        gradients(t, inner[1], slabs)
        return carry

    def outer_render(t, carry):
        value = over(render(t, 0, inner[0]), [picture[t, k] for k in range(4)])
        value = over(value, render(t, inner[1], slabs))
        for k in range(4):
            picture[t, k] = value[k]
        return carry

    def swap(level, other, part, sender):
        radix, stride, _, _ = levels[level]
        digit = depth // stride % radix
        source, slot = (other, digit) if sender else (digit, other)
        return pltpu.make_async_remote_copy(
            src_ref=sent[level].at[source, part],
            dst_ref=got[level].at[slot, part],
            send_sem=swap_send.at[level, source, part],
            recv_sem=swap_recv.at[level, slot, part],
            device_id=(depth + (other - digit) * stride, strip),
            device_id_type=MESH,
        )

    def dispatch(level, j, part):
        radix, stride, _, _ = levels[level]
        digit = depth // stride % radix

        @pl.when(digit != j)
        def _():
            swap(level, j, part, True).start()

        @pl.when(digit == j)
        def _():
            got[level][j, part] = sent[level][j, part]

    def blocks_of(level, j, part):
        radix, _, _, width = levels[level]
        blocks = [q * radix + j for q in range(width // block)]
        if width >= LANES:
            each = LANES // block
            blocks = blocks[part * each:(part + 1) * each]
        return blocks

    def fill(level, j, part, tile_of):
        width = levels[level][3]
        per, _ = piece_tiles(width)
        count = -(-4 // per)
        for c in range(count):
            sent[level][j, part, c] = place(
                [
                    (
                        tile_of(k, b * block // LANES), b * block % LANES,
                        (k - c * per) * width % LANES + i * block, block,
                    )
                    for k in range(c * per, min(4, (c + 1) * per))
                    for i, b in enumerate(blocks_of(level, j, part))
                ],
                lane,
            )

    for c in range(stages):
        wait_halos(c, over_strip)
    lax.fori_loop(0, tiles, inner_field, 0)
    lax.fori_loop(0, tiles, inner_render, 0)

    for c in range(stages):
        leave_halos(c, over_depth)
        if c + 1 < stages:
            start_halos(c + 1, over_depth)
        wait_halos(c, over_depth)
        lax.fori_loop(starts[c], ends[c], outer_field, 0)
        lax.fori_loop(c * per_stage, (c + 1) * per_stage, outer_render, 0)
        for j in range(first[0]):
            fill(0, j, c, lambda k, t: picture[t, k])
            dispatch(0, j, c)

    current = []
    for level, (radix, stride, held, width) in enumerate(levels):
        per, _ = piece_tiles(width)
        digit = depth // stride % radix
        current, gone = [], set()
        for part in range(max(1, width // LANES)):
            for step in range(1, radix):
                swap(level, (digit + step) % radix, part, False).wait_recv()

            def channel(j, k):
                tile = got[level][j, part, k // per]
                shift = -(k % per) * width % LANES
                return pltpu.roll(tile, shift, 1) if shift else tile

            value = [channel(0, k) for k in range(4)]
            for j in range(1, radix):
                value = over(value, [channel(j, k) for k in range(4)])
            current.append(value)
            if level + 1 < len(levels):
                following, _, _, narrower = levels[level + 1]
                for j in range(following):
                    for later in range(max(1, narrower // LANES)):
                        needed = {b * block // LANES for b in blocks_of(level + 1, j, later)}
                        if (j, later) not in gone and max(needed) <= part:
                            gone.add((j, later))
                            fill(level + 1, j, later, lambda k, t: current[t][k])
                            dispatch(level + 1, j, later)

    for k in range(4):
        out_ref[k] = current[0][k][:, :block]

    for c in range(stages):
        leave_halos(c, over_strip)
    for level, (radix, stride, _, width) in enumerate(levels):
        digit = depth // stride % radix
        for part in range(max(1, width // LANES)):
            for step in range(1, radix):
                swap(level, (digit + step) % radix, part, True).wait_send()


def local(volume, extinction, color_map, light_direction):
    rows, slabs, columns = volume.shape
    groups, strips = lax.axis_size("depth"), lax.axis_size("strip")
    tiles, block = columns // LANES, columns // groups
    levels = plan(groups, columns)
    stages = max(1, levels[0][3] // LANES)
    f32 = jnp.float32
    buffers = []
    for radix, _, _, width in levels:
        parts = max(1, width // LANES)
        buffers.append(pltpu.VMEM((radix, parts, piece_tiles(width)[1] // parts, rows, LANES), f32))
    most = max(max(1, width // LANES) for _, _, _, width in levels)
    image = pl.pallas_call(
        functools.partial(kernel, groups, strips, rows, slabs, columns),
        out_shape=jax.ShapeDtypeStruct((4, rows, block), f32),
        in_specs=[pl.BlockSpec(memory_space=pl.ANY)] * 4,
        out_specs=pl.BlockSpec(memory_space=pltpu.VMEM),
        scratch_shapes=[
            pltpu.SMEM((1,), f32),
            pltpu.SMEM((2, 3), f32),
            pltpu.SMEM((3,), f32),
            pltpu.VMEM((tiles, rows * slabs, LANES), f32),
            pltpu.VMEM((tiles, slabs + 4, rows + 2 * EDGE, LANES), f32),
            pltpu.VMEM((tiles, slabs + 2, rows + 8, LANES), f32),
            pltpu.VMEM((tiles + 1, slabs, rows, LANES), f32),
            pltpu.VMEM((tiles + 1, slabs, rows, LANES), f32),
            pltpu.VMEM((tiles, 4, rows, LANES), f32),
            *buffers,
            *buffers,
            pltpu.SemaphoreType.DMA((tiles,)),
            pltpu.SemaphoreType.DMA((3,)),
            pltpu.SemaphoreType.DMA((stages, len(SIDES))),
            pltpu.SemaphoreType.DMA((stages, len(SIDES))),
            pltpu.SemaphoreType.DMA((len(levels), 4, most)),
            pltpu.SemaphoreType.DMA((len(levels), 4, most)),
        ],
        compiler_params=pltpu.CompilerParams(
            collective_id=0, has_side_effects=True, vmem_limit_bytes=55000 * 1024
        ),
    )(extinction, color_map.T, light_direction, volume.reshape(rows * slabs, columns))
    last = lax.broadcasted_iota(jnp.int32, image.shape, 0) == 3
    return jnp.where(last, 1.0 - image, image)


def solution(mesh):
    in_specs = (P("strip", "depth", None), P(), P(), P())
    out_specs = P(None, "strip", "depth")
    return jax.shard_map(local, mesh=mesh, in_specs=in_specs, out_specs=out_specs, check_vma=False)
```
